256 devices in a mesh: slab: 32 (over z, y_lo, core), sub: 8 (over x, y_hi).
Axes of the slice: x: 4, y: 4 (y_hi: 2, y_lo: 2; y = y_hi * 2 + y_lo), z: 8, core: 2. Of those that a mesh axis runs over, the one named last changes fastest.
Arguments:
- positions: float32 [3, 32768], P(None, ('slab', 'sub')), may hold values from 0 to 1
- velocities: float32 [3, 32768], P(None, ('slab', 'sub'))
- species: int32 [32768], P(('slab', 'sub')), may hold values from 0 to 7
- ghost_species: int32 [49152], P(('slab', 'sub')), may hold values from 0 to 7, as said below
- neighbours: int32 [20, 32768], P(None, ('slab', 'sub')), may hold values from 0 to 319, as said below
- slot_mask: int32 [20, 32768], P(None, ('slab', 'sub')), may hold values from 0 to 1, as said below
- edge_vectors: float32 [3, 20, 32768], P(None, None, ('slab', 'sub')), may hold values from -4.8 to 4.8, as said below
- send_slab: int32 [2, 12288], P(None, ('slab', 'sub')), may hold values from 0 to 127, as said below
- send_sub: int32 [2, 12288], P(None, ('slab', 'sub')), may hold values from 0 to 127, as said below
- migrants: int32 [4, 1024], P(None, ('slab', 'sub')), may hold values from 0 to 127, as said below
- embedding: float32 [8, 128], replicated, may hold values from -6 to 6
- energy_shift: float32 [8], replicated, may hold values from -4 to 4
- masses: float32 [8], replicated, may hold values from 0.5 to 4
- radial_one_in: float32 [64, 8], replicated, may hold values from -2 to 2
- radial_one_mid: float32 [2, 64, 64], replicated, may hold values from -0.75 to 0.75
- radial_one_out: float32 [256, 64], replicated, may hold values from -0.75 to 0.75
- node_one: float32 [6, 128, 128], replicated, may hold values from -0.5 to 0.5
- radial_two_in: float32 [64, 8], replicated, may hold values from -2 to 2
- radial_two_mid: float32 [2, 64, 64], replicated, may hold values from -0.75 to 0.75
- radial_two_out: float32 [512, 64], replicated, may hold values from -0.75 to 0.75
- node_two: float32 [5, 128, 128], replicated, may hold values from -0.5 to 0.5
- readout_linear: float32 [128], replicated, may hold values from -0.5 to 0.5
- readout_hidden: float32 [16, 128], replicated, may hold values from -0.5 to 0.5
- readout_out: float32 [16], replicated, may hold values from -1.5 to 1.5
- box_matrix: float32 [3, 3], replicated, as said below
- box_velocity: float32 [3, 3], replicated, may hold values from -3 to 3
Outputs:
- atom_energy: float32 [32768], P(('slab', 'sub'))
- forces: float32 [3, 32768], P(None, ('slab', 'sub'))
- new_velocities: float32 [3, 32768], P(None, ('slab', 'sub'))
- new_positions: float32 [3, 32768], P(None, ('slab', 'sub'))
- arrivals: float32 [6, 4096], P(None, ('slab', 'sub'))
- new_box: float32 [3, 3], replicated
- new_box_velocity: float32 [3, 3], replicated
The draws below stay inside these ranges and needn't reach their ends.
Inputs may be any that keep to these rules, and one draw needn't show every extreme that they name: `neighbours`: the 20 entries of an atom are distinct extended rows of its device. `slot_mask`: live slots of an atom come first; every atom has 10 to 20 live slots and the first atom of each device has all 20. `edge_vectors`: every edge vector has a length between 1.8 and 4.8. `send_slab`: each row holds, for each device, 48 distinct own atoms; row 0 goes to slab index - 1, row 1 to slab index + 1. `send_sub`: each row holds, for each device, 48 distinct own atoms; row 0 goes to sub index - 1, row 1 to sub index + 1. `migrants`: for each device the four rows hold 16 distinct own atoms, moving to slab index - 1, slab index + 1, sub index - 1 and sub index + 1. `ghost_species`: each ghost row holds the species of the atom that the send lists deliver to it. `box_matrix`: the diagonal dominates each row, so the determinant is positive.
All inputs are finite; a program needn't handle non-finite values.
Results may differ from the reference program's by a relative error of at most 0.000061.
Values sent between devices are 32-bit elements; how exact they have to be, the bound alone decides.
A program may use at most 128 MiB of HBM per device.

```python
import math
import jax
import jax.numpy as jnp
from jax import lax

C = 128
RH = 64
NB = 8
RO = 16
NSPEC = 8
SLOTS = 20
ATOMS = 128
MIG = 4
GHOST_SLAB = 48
GHOST_SUB = 48
EXT_ROWS = 320
SLAB_COUNT = 32
SUB_COUNT = 8
ATOMS_ALL = 32768


def layout_lists(key):
    devices = SLAB_COUNT * SUB_COUNT
    key_species, key_slab, key_sub = jax.random.split(key, 3)
    species = jax.random.randint(key_species, (devices, ATOMS), 0, NSPEC, dtype=jnp.int32)
    slab_keys = jax.random.split(key_slab, 2 * devices)
    slab_lists = jax.vmap(lambda single: jax.random.permutation(single, ATOMS)[:GHOST_SLAB])(slab_keys).reshape(2, devices, GHOST_SLAB)
    sub_keys = jax.random.split(key_sub, 2 * devices)
    sub_lists = jax.vmap(lambda single: jax.random.permutation(single, ATOMS)[:GHOST_SUB])(sub_keys).reshape(2, devices, GHOST_SUB)
    return (species, slab_lists.astype(jnp.int32), sub_lists.astype(jnp.int32))


def draw_species(key, part):
    species, slab_lists, sub_lists = layout_lists(key)
    return species.reshape(-1)


def draw_send_slab(key, part):
    species, slab_lists, sub_lists = layout_lists(key)
    return slab_lists.reshape(2, -1)


def draw_send_sub(key, part):
    species, slab_lists, sub_lists = layout_lists(key)
    return sub_lists.reshape(2, -1)


def draw_ghost_species(key, part):
    species, slab_lists, sub_lists = layout_lists(key)
    devices = SLAB_COUNT * SUB_COUNT
    index = jnp.arange(devices).astype(jnp.int32)
    slab_at = index // SUB_COUNT
    sub_at = index % SUB_COUNT
    slab_prev = (slab_at - 1) % SLAB_COUNT * SUB_COUNT + sub_at
    slab_next = (slab_at + 1) % SLAB_COUNT * SUB_COUNT + sub_at
    sub_prev = slab_at * SUB_COUNT + (sub_at - 1) % SUB_COUNT
    sub_next = slab_at * SUB_COUNT + (sub_at + 1) % SUB_COUNT
    blocks = [jnp.take_along_axis(species[source], lists[source], axis=1) for source, lists in ((slab_prev, slab_lists[1]), (slab_next, slab_lists[0]), (sub_prev, sub_lists[1]), (sub_next, sub_lists[0]))]
    return jnp.concatenate(blocks, axis=1).reshape(-1)


def draw_neighbours(key, part):
    key = jax.random.fold_in(key, 11)
    row_keys = jax.random.split(key, ATOMS_ALL)
    picks = jax.vmap(lambda single: jax.random.permutation(single, EXT_ROWS)[:SLOTS])(row_keys)
    return jnp.transpose(picks).astype(jnp.int32)


def draw_slot_mask(key, part):
    key = jax.random.fold_in(key, 12)
    counts = jax.random.randint(key, (ATOMS_ALL,), SLOTS // 2, SLOTS + 1, dtype=jnp.int32)
    counts = counts.at[::ATOMS].set(SLOTS)
    slots_index = jnp.arange(SLOTS).astype(jnp.int32)[:, None]
    return (slots_index < counts[None, :]).astype(jnp.int32)


def draw_edge_vectors(key, part):
    key = jax.random.fold_in(key, 13)
    key_direction, key_length = jax.random.split(key)
    direction = jax.random.normal(key_direction, (3, SLOTS, ATOMS_ALL), jnp.float32)
    length = jax.random.uniform(key_length, (SLOTS, ATOMS_ALL), jnp.float32, 1.8, 4.8)
    magnitude = jnp.maximum(jnp.sqrt(jnp.sum(direction * direction, axis=0)), 1e-06)
    return direction / magnitude[None] * length[None]


def draw_migrants(key, part):
    key = jax.random.fold_in(key, 14)
    devices = SLAB_COUNT * SUB_COUNT
    device_keys = jax.random.split(key, devices)
    picks = jax.vmap(lambda single: jax.random.permutation(single, ATOMS)[:4 * MIG])(device_keys)
    return picks.reshape(devices, 4, MIG).transpose(1, 0, 2).reshape(4, -1).astype(jnp.int32)


def draw_velocities(key, part):
    key = jax.random.fold_in(key, 15)
    atom_index = jnp.arange(ATOMS_ALL).astype(jnp.int32)
    slab_at = (atom_index // (ATOMS * SUB_COUNT)).astype(jnp.float32)
    ramp = slab_at / max(SLAB_COUNT - 1, 1)
    heat = 1.0 + 2.0 * ramp
    noise = jax.random.normal(key, (3, ATOMS_ALL), jnp.float32)
    return noise * jnp.sqrt(heat)[None, :]


def draw_box_matrix(key, part):
    key = jax.random.fold_in(key, 16)
    key_length, key_slant = jax.random.split(key)
    side_length = (ATOMS_ALL / 1.024) ** (1.0 / 3.0)
    slant_range = 0.1
    lengths = jnp.array([side_length, side_length, 4.0 * side_length], jnp.float32) * jax.random.uniform(key_length, (3,), jnp.float32, 0.9, 1.1)
    slanted = jax.random.uniform(key_slant, (3, 3), jnp.float32, -slant_range, slant_range) * side_length
    return slanted * (1.0 - jnp.eye(3, dtype=jnp.float32)) + jnp.diag(lengths)


def shard_levels(own_key, extent, cuts, low, top_value):
    def one(position, blocks):
        draws = jax.random.uniform(jax.random.fold_in(jax.random.fold_in(own_key, 6), position), (blocks,), jnp.float32, low / len(cuts), top_value / len(cuts))
        return jnp.repeat(jnp.exp(draws), extent[position] // blocks).reshape((-1,) + (1,) * (len(extent) - position - 1))

    factor_of = one(*cuts[0])
    for cut in cuts[1:]:
        factor_of = factor_of * one(*cut)
    return factor_of


def scatter_about(rng, shape, spread, most, held_as=jnp.bfloat16):
    values = jax.random.normal(rng, shape, jnp.float32) * spread
    return jnp.minimum(jnp.maximum(values, -most), most).astype(held_as)


def setup_inputs(seed: int = 0) -> dict:
    seeds = jax.random.split(jax.random.key(seed), 27)
    positions = jnp.clip(1.0 * jax.random.uniform(seeds[0], (3, ATOMS_ALL), jnp.float32) ** shard_levels(seeds[0], (3, ATOMS_ALL), ((1, 256),), -0.2, 0.2), 0.0, 1.0)
    velocities = draw_velocities(jax.random.fold_in(seeds[26], 71), 0)
    species = draw_species(jax.random.fold_in(seeds[26], 71), 0)
    ghost_species = draw_ghost_species(jax.random.fold_in(seeds[26], 71), 0)
    neighbours = draw_neighbours(jax.random.fold_in(seeds[26], 71), 0)
    slot_mask = draw_slot_mask(jax.random.fold_in(seeds[26], 71), 0)
    edge_vectors = draw_edge_vectors(jax.random.fold_in(seeds[26], 71), 0)
    send_slab = draw_send_slab(jax.random.fold_in(seeds[26], 71), 0)
    send_sub = draw_send_sub(jax.random.fold_in(seeds[26], 71), 0)
    migrants = draw_migrants(jax.random.fold_in(seeds[26], 71), 0)
    embedding = scatter_about(seeds[10], (NSPEC, C), 1.0, 6.0, jnp.float32)
    energy_shift = scatter_about(seeds[11], (NSPEC,), 1.0, 4.0, jnp.float32)
    masses = jnp.clip(jnp.exp(jax.random.uniform(seeds[12], (NSPEC,), jnp.float32, math.log(0.5), math.log(4.0))), 0.5, 4.0)
    radial_one_in = scatter_about(seeds[13], (RH, NB), NB ** -0.5, 2.0, jnp.float32)
    radial_one_mid = scatter_about(seeds[14], (2, RH, RH), RH ** -0.5, 0.75, jnp.float32)
    radial_one_out = scatter_about(seeds[15], (2 * C, RH), RH ** -0.5, 0.75, jnp.float32)
    node_one = scatter_about(seeds[16], (6, C, C), C ** -0.5, 0.5, jnp.float32)
    radial_two_in = scatter_about(seeds[17], (RH, NB), NB ** -0.5, 2.0, jnp.float32)
    radial_two_mid = scatter_about(seeds[18], (2, RH, RH), RH ** -0.5, 0.75, jnp.float32)
    radial_two_out = scatter_about(seeds[19], (4 * C, RH), RH ** -0.5, 0.75, jnp.float32)
    node_two = scatter_about(seeds[20], (5, C, C), C ** -0.5, 0.5, jnp.float32)
    readout_linear = scatter_about(seeds[21], (C,), C ** -0.5, 0.5, jnp.float32)
    readout_hidden = scatter_about(seeds[22], (RO, C), C ** -0.5, 0.5, jnp.float32)
    readout_out = scatter_about(seeds[23], (RO,), RO ** -0.5, 1.5, jnp.float32)
    box_matrix = draw_box_matrix(jax.random.fold_in(seeds[26], 71), 0)
    box_velocity = scatter_about(seeds[25], (3, 3), 0.3, 3.0, jnp.float32)
    return {"positions": positions, "velocities": velocities, "species": species, "ghost_species": ghost_species, "neighbours": neighbours, "slot_mask": slot_mask, "edge_vectors": edge_vectors, "send_slab": send_slab, "send_sub": send_sub, "migrants": migrants, "embedding": embedding, "energy_shift": energy_shift, "masses": masses, "radial_one_in": radial_one_in, "radial_one_mid": radial_one_mid, "radial_one_out": radial_one_out, "node_one": node_one, "radial_two_in": radial_two_in, "radial_two_mid": radial_two_mid, "radial_two_out": radial_two_out, "node_two": node_two, "readout_linear": readout_linear, "readout_hidden": readout_hidden, "readout_out": readout_out, "box_matrix": box_matrix, "box_velocity": box_velocity}


cutoff = 5.0
neighbor_norm = 0.125
time_step = 0.5
outside_pressure = 0.5
box_mass = 0.125
highest = lax.Precision.HIGHEST

def radial(distance, radial_in, radial_mid, radial_out):
    scaled = distance / cutoff
    orders = jnp.arange(1, radial_in.shape[1] + 1).astype(jnp.float32)[:, None]
    envelope = 1.0 - 28.0 * scaled ** 6 + 48.0 * scaled ** 7 - 21.0 * scaled ** 8
    basis = jnp.sqrt(2.0 / cutoff) * jnp.sin(orders * jnp.pi * scaled) / distance * envelope
    hidden = jax.nn.silu(jnp.dot(radial_in, basis, precision=highest))
    hidden = jax.nn.silu(jnp.dot(radial_mid[0], hidden, precision=highest))
    hidden = jax.nn.silu(jnp.dot(radial_mid[1], hidden, precision=highest))
    return jnp.dot(radial_out, hidden, precision=highest)

def geometry(edges):
    flat = edges.reshape(3, -1)
    distance = jnp.sqrt(lax.optimization_barrier(jnp.sum(flat * flat, axis=0)))
    return (distance, flat / distance)

def slot_sum(values, atoms):
    return values.reshape(values.shape[:-1] + (-1, atoms)).sum(axis=-2)

def layer_one(edges, weights_edge, neighbour_rows, first_table, radial_in, radial_mid, radial_out, node):
    atoms = edges.shape[2]
    width = node.shape[1]
    distance, unit = geometry(edges)
    radial_weights = radial(distance, radial_in, radial_mid, radial_out)
    lifted = jnp.dot(node[0], first_table, precision=highest)
    picked = lifted[:, neighbour_rows] * weights_edge
    scalar_sum = slot_sum(radial_weights[:width] * picked, atoms)
    vector_sum = slot_sum(unit[:, None, :] * (radial_weights[width:] * picked)[None], atoms)
    own = first_table[:, :atoms]
    squares = lax.optimization_barrier(jnp.sum(vector_sum * vector_sum, axis=0))
    scalars = own + jnp.dot(node[1], scalar_sum, precision=highest) + jnp.dot(node[2], scalar_sum * scalar_sum, precision=highest) + jnp.dot(node[3], squares, precision=highest)
    vectors = jnp.einsum('cd,xda->xca', node[4], vector_sum, precision=highest) + jnp.dot(node[5], scalar_sum, precision=highest)[None] * vector_sum
    return jnp.concatenate([scalars, vectors.reshape(3 * width, atoms)], axis=0)

def layer_two(edges, weights_edge, neighbour_rows, table, radial_in, radial_mid, radial_out, node, shift_own, readout_linear, readout_hidden, readout_out):
    atoms = edges.shape[2]
    width = node.shape[1]
    distance, unit = geometry(edges)
    radial_weights = radial(distance, radial_in, radial_mid, radial_out)
    scalars = table[:width]
    vectors = table[width:].reshape(3, width, -1)
    lifted = jnp.dot(node[0], scalars, precision=highest)
    turned = jnp.einsum('cd,xde->xce', node[1], vectors, precision=highest)
    picked = lifted[:, neighbour_rows] * weights_edge
    picked_vector = turned[:, :, neighbour_rows] * weights_edge
    along = lax.optimization_barrier(jnp.sum(picked_vector * unit[:, None, :], axis=0))
    scalar_sum = slot_sum(radial_weights[:width] * picked + radial_weights[3 * width:] * along, atoms)
    vector_sum = slot_sum((radial_weights[width:2 * width] * picked)[None] * unit[:, None, :] + radial_weights[2 * width:3 * width][None] * picked_vector, atoms)
    own = scalars[:, :atoms]
    squares = lax.optimization_barrier(jnp.sum(vector_sum * vector_sum, axis=0))
    second = own + jnp.dot(node[2], scalar_sum, precision=highest) + jnp.dot(node[3], scalar_sum * scalar_sum, precision=highest) + jnp.dot(node[4], squares, precision=highest)
    hidden = jax.nn.silu(jnp.dot(readout_hidden, second, precision=highest))
    return shift_own + jnp.dot(readout_linear, own, precision=highest) + jnp.dot(readout_out, hidden, precision=highest)

def determinant(matrix):
    return matrix[0, 0] * (matrix[1, 1] * matrix[2, 2] - matrix[1, 2] * matrix[2, 1]) - matrix[0, 1] * (matrix[1, 0] * matrix[2, 2] - matrix[1, 2] * matrix[2, 0]) + matrix[0, 2] * (matrix[1, 0] * matrix[2, 1] - matrix[1, 1] * matrix[2, 0])

def inverse(matrix):
    cofactors = []
    for row_index in range(3):
        entries = []
        for column_index in range(3):
            entries.append(matrix[(row_index + 1) % 3, (column_index + 1) % 3] * matrix[(row_index + 2) % 3, (column_index + 2) % 3] - matrix[(row_index + 1) % 3, (column_index + 2) % 3] * matrix[(row_index + 2) % 3, (column_index + 1) % 3])
        cofactors.append(jnp.stack(entries))
    return jnp.transpose(jnp.stack(cofactors)) / determinant(matrix)

def drift(inverse_box, moving):
    return lax.optimization_barrier(jnp.sum(inverse_box[:, :, None] * moving[None, :, :], axis=1))

def neighbour_devices():
    index = jnp.arange(SLAB_COUNT * SUB_COUNT).astype(jnp.int32)
    slab_at = index // SUB_COUNT
    sub_at = index % SUB_COUNT
    slab_prev = (slab_at - 1) % SLAB_COUNT * SUB_COUNT + sub_at
    slab_next = (slab_at + 1) % SLAB_COUNT * SUB_COUNT + sub_at
    sub_prev = slab_at * SUB_COUNT + (sub_at - 1) % SUB_COUNT
    sub_next = slab_at * SUB_COUNT + (sub_at + 1) % SUB_COUNT
    return (slab_prev, slab_next, sub_prev, sub_next)

def reference(positions, velocities, species, ghost_species, neighbours, slot_mask, edge_vectors, send_slab, send_sub, migrants, embedding, energy_shift, masses, radial_one_in, radial_one_mid, radial_one_out, node_one, radial_two_in, radial_two_mid, radial_two_out, node_two, readout_linear, readout_hidden, readout_out, box_matrix, box_velocity):
    devices = SLAB_COUNT * SUB_COUNT
    atoms = ATOMS
    width = node_one.shape[1]
    slab_prev, slab_next, sub_prev, sub_next = neighbour_devices()
    own_ids = jnp.arange(devices * atoms).astype(jnp.int32).reshape(devices, atoms)
    slab_lists = send_slab.reshape(2, devices, -1)
    sub_lists = send_sub.reshape(2, devices, -1)
    extended_ids = jnp.concatenate([own_ids, slab_prev[:, None] * atoms + slab_lists[1][slab_prev], slab_next[:, None] * atoms + slab_lists[0][slab_next], sub_prev[:, None] * atoms + sub_lists[1][sub_prev], sub_next[:, None] * atoms + sub_lists[0][sub_next]], axis=1)
    edges_dev = edge_vectors.reshape(3, SLOTS, devices, atoms).transpose(2, 0, 1, 3)
    rows_dev = neighbours.reshape(SLOTS, devices, atoms).transpose(1, 0, 2).reshape(devices, -1)
    weights_dev = slot_mask.reshape(SLOTS, devices, atoms).transpose(1, 0, 2).reshape(devices, -1).astype(jnp.float32) * neighbor_norm
    species_ext = jnp.concatenate([species.reshape(devices, atoms), ghost_species.reshape(devices, -1)], axis=1)
    first_dev = jnp.transpose(embedding)[:, species_ext].transpose(1, 0, 2)
    shift_dev = energy_shift[species].reshape(devices, atoms)

    def group(values):
        return values.reshape((devices // 8, 8) + values.shape[1:])

    def energies_of(edges):

        def first_one(block):
            return layer_one(block[0], block[1], block[2], block[3], radial_one_in, radial_one_mid, radial_one_out, node_one)
        features = lax.map(jax.checkpoint(jax.vmap(first_one)), (group(edges), group(weights_dev), group(rows_dev), group(first_dev)))
        features = features.reshape(devices, 4 * width, atoms)
        table = features.transpose(1, 0, 2).reshape(4 * width, devices * atoms)

        def second_one(block):
            return layer_two(block[0], block[1], block[2], table[:, block[3]], radial_two_in, radial_two_mid, radial_two_out, node_two, block[4], readout_linear, readout_hidden, readout_out)
        energies = lax.map(jax.checkpoint(jax.vmap(second_one)), (group(edges), group(weights_dev), group(rows_dev), group(extended_ids), group(shift_dev)))
        return energies.reshape(devices * atoms)
    atom_energy, pullback = jax.vjp(energies_of, edges_dev)
    gradient, = pullback(jnp.ones_like(atom_energy))
    gradient_t = gradient.transpose(1, 2, 0, 3)
    gradient_flat = gradient_t.reshape(3, -1)
    forces = lax.optimization_barrier(jnp.sum(gradient_t, axis=1)).reshape(3, -1)
    global_rows = jax.vmap(lambda identity, picks: identity[picks])(extended_ids, rows_dev)
    global_rows = global_rows.reshape(devices, SLOTS, atoms).transpose(1, 0, 2).reshape(-1)
    forces = forces.at[:, global_rows].add(-gradient_flat)
    mass = masses[species]
    new_velocities = velocities + time_step * forces / mass[None]
    kinetic = jnp.einsum('ai,bi->ab', new_velocities * mass[None], new_velocities, precision=highest)
    virial = jnp.einsum('ae,be->ab', edge_vectors.reshape(3, -1), gradient_flat, precision=highest)
    stress = kinetic - virial
    volume = determinant(box_matrix)
    identity_three = jnp.eye(3, dtype=jnp.float32)
    push = jnp.dot(stress - outside_pressure * volume * identity_three, jnp.transpose(inverse(box_matrix)), precision=highest)
    new_box_velocity = box_velocity + time_step * push / (box_mass * devices * atoms)
    new_box = box_matrix + time_step * new_box_velocity
    new_positions = positions + time_step * drift(inverse(new_box), new_velocities)
    moving = migrants.reshape(4, devices, -1)
    come_ids = jnp.concatenate([slab_prev[:, None] * atoms + moving[1][slab_prev], slab_next[:, None] * atoms + moving[0][slab_next], sub_prev[:, None] * atoms + moving[3][sub_prev], sub_next[:, None] * atoms + moving[2][sub_next]], axis=1).reshape(-1)
    arrivals = jnp.concatenate([new_positions, new_velocities], axis=0)[:, come_ids]
    return (atom_energy, forces, new_velocities, new_positions, arrivals, new_box, new_box_velocity)
```

```python
import functools

import jax
import jax.numpy as jnp
from jax import lax
from jax.experimental import pallas as pl
from jax.experimental.pallas import tpu as pltpu
from jax.sharding import PartitionSpec as P

MESH = pl.DeviceIdType.MESH
F32 = jnp.float32
BF16 = jnp.bfloat16
HIGHEST = lax.Precision.HIGHEST

cutoff = 5.0
neighbor_norm = 0.125
time_step = 0.5
outside_pressure = 0.5
box_mass = 0.125

C = 128
A = 128
K = 20
GH = 48
EXT = A + 4 * GH
CH = 4
NCH = K // CH
W = CH * A
E = K * A
RH = 64
LO = 2


def split2(x):
    high = x.astype(BF16)
    return high, (x - high.astype(F32)).astype(BF16)


def split3(x):
    high = x.astype(BF16).astype(F32)
    rest = x - high
    middle = rest.astype(BF16).astype(F32)
    return high, middle, rest - middle


def stack_left(weights):
    high, low = split2(weights)
    return jnp.concatenate([high, high, low], axis=1)


def stack_right(values):
    high, low = split2(values)
    return jnp.concatenate([high, low, high], axis=0)


def mm(left, right):
    return jnp.dot(left, right, preferred_element_type=F32)


def mm_nt(left, right):
    return lax.dot_general(left, right, (((1,), (1,)), ((), ())), preferred_element_type=F32)


def mix(weights, values):
    return mm(stack_left(weights), stack_right(values))


def logistic(x):
    return 1.0 / (1.0 + jnp.exp(-x))


def radial_net(start, win, mid0, mid1, out):
    pre = mm(win, start)
    for after in (mid0, mid1, out):
        half = pre.shape[1] // 2
        value, slope = pre[:, :half], pre[:, half:]
        gate = logistic(value)
        active = value * gate
        moved = (gate + active * (1.0 - gate)) * slope
        pre = mm(after, stack_right(jnp.concatenate([active, moved], axis=1)))
    return pre


def kernel(slabs, subs, *refs):
    (
        positions, velocities, species, ghost_species, neighbours, slot_mask, edges, send_slab, send_sub, migrants,
        embedding, energy_shift, masses, one_in, one_mid, one_out, node_one, two_in, two_mid, two_out, node_two,
        readout_linear, readout_hidden, readout_out, box_matrix, box_velocity,
        energy_out, forces_out, velocities_out, positions_out, arrivals_out, box_out, box_velocity_out,
        lists, geo, basis, hot, kept1, radial1, radial2, sums, pairs, table, parts, gather_parts,
        packed, gflat, send_a, recv_a, scat, recv_b, push, recv_c, send_d, recv_d, stage1, stage2,
        part1, part2, send_sem, recv_sem, sum_send, sum_recv,
    ) = refs
    slab, sub = lax.axis_index("slab"), lax.axis_index("sub")
    low, high = lax.rem(slab, LO), slab // LO
    many1, many2 = LO * subs, slabs // LO
    mine1 = low * subs + sub

    def first_peer(step):
        flat = lax.rem(mine1 + step, many1)
        return (high * LO + flat // subs, lax.rem(flat, subs))

    def second_peer(step):
        return (lax.rem(high + step, many2) * LO + low, sub)

    around = (
        (lax.rem(slab + slabs - 1, slabs), sub),
        (lax.rem(slab + 1, slabs), sub),
        (slab, lax.rem(sub + subs - 1, subs)),
        (slab, lax.rem(sub + 1, subs)),
    )
    barrier = pltpu.get_barrier_semaphore()

    def greet(device):
        pl.semaphore_signal(barrier, inc=1, device_id=device, device_id_type=MESH)

    for device in around:
        greet(device)

    @pl.loop(1, many1)
    def _(step):
        greet(first_peer(step))

    @pl.loop(1, many2)
    def _(step):
        greet(second_peer(step))

    def exchange(number, source, target):
        copies = []
        for block in range(4):
            copy = pltpu.make_async_remote_copy(
                src_ref=source(block),
                dst_ref=target(block ^ 1),
                send_sem=send_sem.at[number, block],
                recv_sem=recv_sem.at[number, block ^ 1],
                device_id=around[block],
                device_id_type=MESH,
            )
            copy.start()
            copies.append(copy)
        return copies

    def rows(block):
        return pl.ds(block * GH, GH)

    lane = lax.broadcasted_iota(jnp.int32, (1, A), 1)

    lists[...] = jnp.zeros_like(lists)
    lists[0:2, 0:GH] = send_slab[...].astype(F32)
    lists[2:4, 0:GH] = send_sub[...].astype(F32)
    columns = lists[...].T
    lanes_f = lax.broadcasted_iota(jnp.int32, (GH, A), 1).astype(F32)
    sent_f = jnp.concatenate(
        [(lanes_f == columns[0:GH, q : q + 1]).astype(F32) for q in range(4)], axis=0
    )
    sent_rows = sent_f.astype(BF16)
    sent_columns = sent_f.T.astype(BF16)

    ex, ey, ez = edges[0], edges[1], edges[2]
    distance = jnp.sqrt(ex * ex + ey * ey + ez * ez)
    inverse_distance = 1.0 / distance
    unit = (ex / distance, ey / distance, ez / distance)
    weight = slot_mask[...].astype(F32) * neighbor_norm
    for row, values in enumerate(unit + (weight, distance, inverse_distance)):
        for k in range(K):
            geo[row : row + 1, k * A : (k + 1) * A] = values[k : k + 1, :]

    kinds = lax.broadcasted_iota(jnp.int32, (8, A), 0)
    own_kind = (kinds == species[...]).astype(F32)
    ghost_kinds = lax.broadcasted_iota(jnp.int32, (8, 4 * GH), 0)
    ghost_kind = (ghost_kinds == ghost_species[...]).astype(F32)
    pad8 = jnp.zeros((8, A), F32)
    own_kind16 = jnp.concatenate([own_kind, pad8], axis=0).astype(BF16)
    ghost_kind16 = jnp.concatenate([ghost_kind, jnp.zeros((8, 4 * GH), F32)], axis=0).astype(BF16)

    orders = (lax.broadcasted_iota(jnp.int32, (8, 1), 0) + 1).astype(F32) * jnp.pi
    scale = jnp.sqrt(2.0 / cutoff).astype(F32)

    one_in_s = jnp.concatenate(
        [part for part in (lambda h, m, l: (h, h, h, m, m, l))(*split3(one_in[...].T))], axis=0
    ).T.astype(BF16)
    two_in_s = jnp.concatenate(
        [part for part in (lambda h, m, l: (h, h, h, m, m, l))(*split3(two_in[...].T))], axis=0
    ).T.astype(BF16)
    one_mid0, one_mid1 = stack_left(one_mid[0]), stack_left(one_mid[1])
    one_out_s = stack_left(one_out[...])

    lifted = lax.dot_general(
        embedding[...], node_one[0], (((1,), (1,)), ((), ())), precision=HIGHEST, preferred_element_type=F32
    )
    lifted_s = jnp.concatenate(list(split3(lifted)) + [pad8], axis=0).T.astype(BF16)

    sums[...] = jnp.zeros_like(sums)

    def lanes_of(chunk):
        return pl.ds(pl.multiple_of(chunk * W, W), W)

    def first_forward(chunk, _):
        here = lanes_of(chunk)
        row_of = lax.broadcasted_iota(jnp.int32, (EXT, A), 0)
        for j in range(CH):
            picked = neighbours[pl.ds(chunk * CH + j, 1), :]
            hot[chunk, :, j * A : (j + 1) * A] = (row_of == picked).astype(F32).astype(BF16)
        d = geo[4:5, here]
        inverse_d = geo[5:6, here]
        x = d / cutoff
        x2 = x * x
        x3 = x2 * x
        x5 = x2 * x3
        x6 = x3 * x3
        envelope = 1.0 - 28.0 * x6 + 48.0 * x6 * x - 21.0 * x6 * x2
        slope = (-168.0 * x5 + 336.0 * x6 - 168.0 * x6 * x) / cutoff
        angle = orders * x
        sine, cosine = jnp.sin(angle), jnp.cos(angle)
        even = scale * inverse_d * envelope
        values = sine * even
        slopes = cosine * (orders / cutoff) * even + sine * (scale * inverse_d * (slope - envelope * inverse_d))
        h, m, l = split3(jnp.concatenate([values, slopes], axis=1))
        start = jnp.concatenate([h, m, l, h, m, h], axis=0).astype(BF16)
        basis[chunk] = start
        radial1[...] = radial_net(start, one_in_s, one_mid0, one_mid1, one_out_s)
        kind = mm(own_kind16, hot[chunk, 0:A, :]) + mm(ghost_kind16, hot[chunk, A:EXT, :])
        kind8 = kind[0:8]
        picked_x = mm(lifted_s, jnp.concatenate([kind8, kind8, kind8, jnp.zeros_like(kind8)], axis=0).astype(BF16))
        total = [jnp.zeros((C, A), F32) for _ in range(4)]
        for j in range(CH):
            cut = slice(j * A, (j + 1) * A)
            far = slice(W + j * A, W + (j + 1) * A)
            at = pl.ds(pl.multiple_of(chunk * W + j * A, A), A)
            wx = picked_x[:, cut] * geo[3:4, at]
            total[0] += radial1[0:C, cut] * wx
            q1 = radial1[C : 2 * C, cut] * wx
            for a in range(3):
                total[a + 1] += geo[a : a + 1, at] * q1
            kept1[chunk, 0:C, cut] = q1
            kept1[chunk, C : 2 * C, cut] = radial1[0:C, far] * wx
            kept1[chunk, 2 * C : 3 * C, cut] = radial1[C : 2 * C, far] * wx
        for a in range(4):
            sums[a] += total[a]
        return 0

    lax.fori_loop(0, NCH, first_forward, 0)

    s0 = mm(
        jnp.concatenate(list(split3(embedding[...])) + [pad8], axis=0).T.astype(BF16),
        jnp.concatenate([own_kind, own_kind, own_kind, pad8], axis=0).astype(BF16),
    )
    a0 = sums[0]
    a1 = [sums[1], sums[2], sums[3]]
    square = a1[0] * a1[0] + a1[1] * a1[1] + a1[2] * a1[2]
    s1 = s0 + mix(node_one[1], a0) + mix(node_one[2], a0 * a0) + mix(node_one[3], square)
    turned = mix(node_one[4], jnp.concatenate(a1, axis=1))
    gate1 = mix(node_one[5], a0)
    v1 = jnp.concatenate([turned[:, a * A : (a + 1) * A] + gate1 * a1[a] for a in range(3)], axis=1)
    lifted_x = mix(node_two[0], s1)
    lifted_y = mix(node_two[1], v1)
    own_table = jnp.concatenate([lifted_x] + [lifted_y[:, a * A : (a + 1) * A] for a in range(3)], axis=0)
    own_high, own_low = split2(own_table)
    send_a[...] = mm_nt(sent_rows, own_high) + mm_nt(sent_rows, own_low)
    table[:, 0:A] = own_high
    table[:, A : 2 * A] = own_low

    pl.semaphore_wait(barrier, 4 + many1 - 1 + many2 - 1)
    copies_a = exchange(0, lambda q: send_a.at[rows(q)], lambda q: recv_a.at[rows(q)])

    two_mid0, two_mid1 = stack_left(two_mid[0]), stack_left(two_mid[1])
    two_out_s = stack_left(two_out[...])

    def second_radial(chunk, _):
        radial2[chunk] = radial_net(basis[chunk], two_in_s, two_mid0, two_mid1, two_out_s)
        return 0

    lax.fori_loop(0, NCH, second_radial, 0)

    for copy in copies_a:
        copy.wait_recv()
    ghost_high, ghost_low = split2(recv_a[...].T)
    gather_parts[:, 0 : 4 * GH] = ghost_high
    gather_parts[:, 4 * GH : 8 * GH] = ghost_low

    sums2 = parts
    sums2[...] = jnp.zeros_like(sums2)

    def second_forward(chunk, _):
        own_hot = hot[chunk, 0:A, :]
        far_hot = hot[chunk, A:EXT, :]
        pairs[chunk] = mm(table[...], jnp.concatenate([own_hot, own_hot], axis=0)) + mm(
            gather_parts[...], jnp.concatenate([far_hot, far_hot], axis=0)
        )
        total = [jnp.zeros((C, A), F32) for _ in range(4)]
        for j in range(CH):
            cut = slice(j * A, (j + 1) * A)
            at = pl.ds(pl.multiple_of(chunk * W + j * A, A), A)
            w = geo[3:4, at]
            u = [geo[a : a + 1, at] for a in range(3)]
            wx = pairs[chunk, 0:C, cut] * w
            wy = [pairs[chunk, (a + 1) * C : (a + 2) * C, cut] * w for a in range(3)]
            along = wy[0] * u[0] + wy[1] * u[1] + wy[2] * u[2]
            total[0] += radial2[chunk, 0:C, cut] * wx + radial2[chunk, 3 * C : 4 * C, cut] * along
            r1x = radial2[chunk, C : 2 * C, cut] * wx
            r2 = radial2[chunk, 2 * C : 3 * C, cut]
            for a in range(3):
                total[a + 1] += r1x * u[a] + r2 * wy[a]
        for a in range(4):
            sums2[a] += total[a]
        return 0

    lax.fori_loop(0, NCH, second_forward, 0)

    b0 = sums2[0]
    b1 = [sums2[1], sums2[2], sums2[3]]
    square2 = b1[0] * b1[0] + b1[1] * b1[1] + b1[2] * b1[2]
    s2 = s1 + mix(node_two[2], b0) + mix(node_two[3], b0 * b0) + mix(node_two[4], square2)
    pre = mix(readout_hidden[...], s2)
    gate2 = logistic(pre)
    hidden = pre * gate2
    linear = jnp.broadcast_to(readout_linear[...], (A, C)).T
    outer = jnp.broadcast_to(readout_out[...], (A, 16)).T
    shift = jnp.zeros((1, A), F32)
    mass = jnp.zeros((1, A), F32)
    for s in range(8):
        shift = jnp.where(species[...] == s, energy_shift[s], shift)
        mass = jnp.where(species[...] == s, masses[s], mass)
    energy_out[...] = (
        shift + jnp.sum(linear * s1, axis=0, keepdims=True) + jnp.sum(outer * hidden, axis=0, keepdims=True)
    )
    back_pre = outer * (gate2 + hidden * (1.0 - gate2))
    back_s2 = mix(readout_hidden[...].T, back_pre)
    back_b0 = mix(node_two[2].T, back_s2) + 2.0 * b0 * mix(node_two[3].T, back_s2)
    back_square2 = 2.0 * mix(node_two[4].T, back_s2)
    sums2[0] = back_b0
    for a in range(3):
        sums2[a + 1] = b1[a] * back_square2

    scat[...] = jnp.zeros_like(scat)

    def second_back(chunk, _):
        for j in range(CH):
            cut = slice(j * A, (j + 1) * A)
            far = slice(W + j * A, W + (j + 1) * A)
            at = pl.ds(pl.multiple_of(chunk * W + j * A, A), A)
            w = geo[3:4, at]
            u = [geo[a : a + 1, at] for a in range(3)]
            wb0 = sums2[0] * w
            wb1 = [sums2[a + 1] * w for a in range(3)]
            dot_u = wb1[0] * u[0] + wb1[1] * u[1] + wb1[2] * u[2]
            back = [radial2[chunk, 0:C, cut] * wb0 + radial2[chunk, C : 2 * C, cut] * dot_u]
            r3b0 = radial2[chunk, 3 * C : 4 * C, cut] * wb0
            r2 = radial2[chunk, 2 * C : 3 * C, cut]
            for a in range(3):
                back.append(r3b0 * u[a] + r2 * wb1[a])
            for a in range(4):
                h, l = split2(back[a])
                kept = slice(a * C, (a + 1) * C)
                packed[kept, cut] = h
                packed[kept, far] = l
        hot_here = hot[chunk]
        scat[...] += mm_nt(hot_here, packed[:, 0:W]) + mm_nt(hot_here, packed[:, W : 2 * W])
        return 0

    lax.fori_loop(0, NCH, second_back, 0)
    copies_b = exchange(1, lambda q: scat.at[pl.ds(A + q * GH, GH)], lambda q: recv_b.at[rows(q)])

    def second_edges(chunk, _):
        for j in range(CH):
            cut = slice(j * A, (j + 1) * A)
            far = slice(W + j * A, W + (j + 1) * A)
            at = pl.ds(pl.multiple_of(chunk * W + j * A, A), A)
            w = geo[3:4, at]
            u = [geo[a : a + 1, at] for a in range(3)]
            k0 = sums2[0]
            k1 = [sums2[a + 1] for a in range(3)]
            x = pairs[chunk, 0:C, cut]
            y = [pairs[chunk, (a + 1) * C : (a + 2) * C, cut] for a in range(3)]
            dot_u = k1[0] * u[0] + k1[1] * u[1] + k1[2] * u[2]
            along = y[0] * u[0] + y[1] * u[1] + y[2] * u[2]
            cross = y[0] * k1[0] + y[1] * k1[1] + y[2] * k1[2]
            stretch = (
                (radial2[chunk, 0:C, far] * k0 + radial2[chunk, C : 2 * C, far] * dot_u) * x
                + radial2[chunk, 3 * C : 4 * C, far] * along * k0
                + radial2[chunk, 2 * C : 3 * C, far] * cross
            )
            gflat[3:4, at] = w * jnp.sum(stretch, axis=0, keepdims=True)
            r3k0 = radial2[chunk, 3 * C : 4 * C, cut] * k0
            r1x = radial2[chunk, C : 2 * C, cut] * x
            for a in range(3):
                gflat[a : a + 1, at] = w * jnp.sum(r3k0 * y[a] + r1x * k1[a], axis=0, keepdims=True)
        return 0

    lax.fori_loop(0, NCH, second_edges, 0)

    for copy in copies_b:
        copy.wait_recv()
    back_high, back_low = split2(recv_b[...])
    back_table = (scat[0:A] + mm(sent_columns, back_high) + mm(sent_columns, back_low)).T
    back_s1 = back_s2 + linear + mix(node_two[0].T, back_table[0:C])
    back_v1 = mix(
        node_two[1].T, jnp.concatenate([back_table[(a + 1) * C : (a + 2) * C] for a in range(3)], axis=1)
    )
    back_turned = mix(node_one[4].T, back_v1)
    back_square = 2.0 * mix(node_one[3].T, back_s1)
    cut_v = [back_v1[:, a * A : (a + 1) * A] for a in range(3)]
    back_gate = a1[0] * cut_v[0] + a1[1] * cut_v[1] + a1[2] * cut_v[2]
    sums[0] = (
        mix(node_one[1].T, back_s1) + 2.0 * a0 * mix(node_one[2].T, back_s1) + mix(node_one[5].T, back_gate)
    )
    for a in range(3):
        sums[a + 1] = back_turned[:, a * A : (a + 1) * A] + gate1 * cut_v[a] + a1[a] * back_square

    push[...] = jnp.zeros_like(push)

    def first_edges(chunk, _):
        pieces = []
        for j in range(CH):
            cut = slice(j * A, (j + 1) * A)
            at = pl.ds(pl.multiple_of(chunk * W + j * A, A), A)
            u = [geo[a : a + 1, at] for a in range(3)]
            inverse_d = geo[5:6, at]
            k1 = [sums[a + 1] for a in range(3)]
            q1 = kept1[chunk, 0:C, cut]
            dot_u = k1[0] * u[0] + k1[1] * u[1] + k1[2] * u[2]
            stretch = gflat[3:4, at] + jnp.sum(
                kept1[chunk, C : 2 * C, cut] * sums[0] + kept1[chunk, 2 * C : 3 * C, cut] * dot_u,
                axis=0,
                keepdims=True,
            )
            turn = [gflat[a : a + 1, at] + jnp.sum(q1 * k1[a], axis=0, keepdims=True) for a in range(3)]
            inward = turn[0] * u[0] + turn[1] * u[1] + turn[2] * u[2]
            radial_part = stretch - inward * inverse_d
            for a in range(3):
                gflat[a : a + 1, at] = radial_part * u[a] + turn[a] * inverse_d
            gflat[3:8, at] = jnp.zeros((5, A), F32)
        g = gflat[:, lanes_of(chunk)]
        g_high = g.astype(BF16).astype(F32)
        both = jnp.concatenate([g_high, g - g_high], axis=0).astype(BF16)
        push[...] += mm_nt(hot[chunk], both)
        return 0

    lax.fori_loop(0, NCH, first_edges, 0)
    pushed = push[...]
    pushed = pushed[:, 0:8] + pushed[:, 8:16]
    push[:, 0:8] = pushed
    copies_c = exchange(2, lambda q: push.at[pl.ds(A + q * GH, GH)], lambda q: recv_c.at[rows(q)])

    own = jnp.zeros((8, A), F32)
    virial = [[jnp.zeros((1, A), F32) for _ in range(3)] for _ in range(3)]
    for k in range(K):
        own += gflat[:, k * A : (k + 1) * A]
        for a in range(3):
            for b in range(3):
                virial[a][b] += edges[a, k : k + 1, :] * gflat[b : b + 1, k * A : (k + 1) * A]
    for copy in copies_c:
        copy.wait_recv()
    come_high, come_low = split2(recv_c[...])
    back_f = (push[0:A] + mm(sent_columns, come_high) + mm(sent_columns, come_low)).T
    forces = own[0:3] - back_f[0:3]
    forces_out[...] = forces
    new_velocities = velocities[...] + time_step * forces / mass
    velocities_out[...] = new_velocities

    order = (1, 0, 3, 2)
    movers = jnp.full((1, A), -1, jnp.int32)
    for q in range(4):
        for j in range(4):
            movers = jnp.where(lane == 4 * q + j, migrants[order[q], j], movers)
    chosen = (lax.broadcasted_iota(jnp.int32, (A, A), 0) == movers).astype(F32).astype(BF16)
    state = jnp.concatenate([positions[...], new_velocities, jnp.zeros((2, A), F32)], axis=0)
    h, m, l = split3(state)
    sent_state = mm(jnp.concatenate([h, m, l, jnp.zeros_like(h)], axis=0).astype(BF16), chosen)
    send_d[...] = sent_state[0:8] + sent_state[8:16] + sent_state[16:24]
    copies_d = exchange(3, lambda q: send_d, lambda q: recv_d.at[q])

    mine = jnp.zeros((1, A), F32)
    for a in range(3):
        for b in range(3):
            term = new_velocities[a : a + 1] * mass * new_velocities[b : b + 1] - virial[a][b]
            mine = jnp.where(lane == 3 * a + b, jnp.sum(term, axis=1, keepdims=True), mine)

    def all_sum(number, value, part, stage, many, me, peer):
        part[...] = value.reshape(1, 1, A)
        stage[pl.ds(me, 1)] = value.reshape(1, 1, A)

        @pl.loop(1, many)
        def _(step):
            pltpu.make_async_remote_copy(
                src_ref=part,
                dst_ref=stage.at[pl.ds(me, 1)],
                send_sem=sum_send.at[number],
                recv_sem=sum_recv.at[number],
                device_id=peer(step),
                device_id_type=MESH,
            ).start()

        whole = stage.at[pl.ds(0, many - 1)]
        pltpu.make_async_copy(whole, whole, sum_recv.at[number]).wait()
        pltpu.make_async_copy(whole, whole, sum_send.at[number]).wait()
        return jnp.sum(stage[...], axis=0)

    near = all_sum(0, mine, part1, stage1, many1, mine1, first_peer)
    stress_row = all_sum(1, near, part2, stage2, many2, high, second_peer)

    def entry(ref, a, b):
        return jnp.full((1, A), ref[a, b], F32)

    def determinant(m):
        return (
            m[0][0] * (m[1][1] * m[2][2] - m[1][2] * m[2][1])
            - m[0][1] * (m[1][0] * m[2][2] - m[1][2] * m[2][0])
            + m[0][2] * (m[1][0] * m[2][1] - m[1][1] * m[2][0])
        )

    def inverse(m):
        det = determinant(m)
        cof = [
            [
                m[(r + 1) % 3][(c + 1) % 3] * m[(r + 2) % 3][(c + 2) % 3]
                - m[(r + 1) % 3][(c + 2) % 3] * m[(r + 2) % 3][(c + 1) % 3]
                for c in range(3)
            ]
            for r in range(3)
        ]
        return [[cof[c][r] / det for c in range(3)] for r in range(3)]

    box = [[entry(box_matrix, a, b) for b in range(3)] for a in range(3)]
    volume = determinant(box)
    inv = inverse(box)
    total_atoms = box_mass * (A * slabs * subs)
    pressed = []
    for a in range(3):
        line = []
        for b in range(3):
            value = jnp.broadcast_to(stress_row[:, 3 * a + b : 3 * a + b + 1], (1, A))
            line.append(value - outside_pressure * volume if a == b else value)
        pressed.append(line)
    box_speed = []
    for a in range(3):
        line = []
        for b in range(3):
            pushed_box = pressed[a][0] * inv[b][0] + pressed[a][1] * inv[b][1] + pressed[a][2] * inv[b][2]
            line.append(entry(box_velocity, a, b) + time_step * pushed_box / total_atoms)
        box_speed.append(line)
    new_box = [[box[a][b] + time_step * box_speed[a][b] for b in range(3)] for a in range(3)]
    new_inverse = inverse(new_box)
    for a in range(3):
        for b in range(3):
            box_out[a : a + 1, b : b + 1] = new_box[a][b][:, 0:1]
            box_velocity_out[a : a + 1, b : b + 1] = box_speed[a][b][:, 0:1]

    def drift(moving):
        return [
            new_inverse[a][0] * moving[0:1] + new_inverse[a][1] * moving[1:2] + new_inverse[a][2] * moving[2:3]
            for a in range(3)
        ]

    moved = drift(new_velocities)
    for a in range(3):
        positions_out[a : a + 1, :] = positions[a : a + 1, :] + time_step * moved[a]
    for copy in copies_d:
        copy.wait_recv()
    come = jnp.where(
        lane < 4, recv_d[0], jnp.where(lane < 8, recv_d[1], jnp.where(lane < 12, recv_d[2], recv_d[3]))
    )
    moved = drift(come[3:6])
    for a in range(3):
        arrivals_out[a : a + 1, :] = (come[a : a + 1] + time_step * moved[a])[:, 0:16]
    arrivals_out[3:6, :] = come[3:6, 0:16]

    for copies in (copies_a, copies_b, copies_c, copies_d):
        for copy in copies:
            copy.wait_send()


def solution(mesh):
    slabs, subs = mesh.shape["slab"], mesh.shape["sub"]
    many1, many2 = LO * subs, slabs // LO
    vmem = pl.BlockSpec(memory_space=pltpu.VMEM)
    smem = pl.BlockSpec(memory_space=pltpu.SMEM)
    in_smem = {9, 11, 12, 24, 25}

    def body(*arrays):
        arrays = list(arrays)
        for position in (2, 3, 21, 23):
            arrays[position] = arrays[position].reshape(1, -1)
        shapes = [(1, A), (3, A), (3, A), (3, A), (6, 16), (3, 3), (3, 3)]
        outs = pl.pallas_call(
            functools.partial(kernel, slabs, subs),
            out_shape=[jax.ShapeDtypeStruct(shape, F32) for shape in shapes],
            in_specs=[smem if i in in_smem else vmem for i in range(26)],
            out_specs=[vmem] * 7,
            scratch_shapes=[
                pltpu.VMEM((8, 128), F32),
                pltpu.VMEM((8, E), F32),
                pltpu.VMEM((NCH, 48, 2 * W), BF16),
                pltpu.VMEM((NCH, EXT, W), BF16),
                pltpu.VMEM((NCH, 3 * C, W), F32),
                pltpu.VMEM((2 * C, 2 * W), F32),
                pltpu.VMEM((NCH, 4 * C, 2 * W), F32),
                pltpu.VMEM((4, C, A), F32),
                pltpu.VMEM((NCH, 4 * C, W), F32),
                pltpu.VMEM((4 * C, 2 * A), BF16),
                pltpu.VMEM((4, C, A), F32),
                pltpu.VMEM((4 * C, 8 * GH), BF16),
                pltpu.VMEM((4 * C, 2 * W), BF16),
                pltpu.VMEM((8, E), F32),
                pltpu.VMEM((4 * GH, 4 * C), F32),
                pltpu.VMEM((4 * GH, 4 * C), F32),
                pltpu.VMEM((EXT, 4 * C), F32),
                pltpu.VMEM((4 * GH, 4 * C), F32),
                pltpu.VMEM((EXT, 16), F32),
                pltpu.VMEM((4 * GH, 16), F32),
                pltpu.VMEM((8, A), F32),
                pltpu.VMEM((4, 8, A), F32),
                pltpu.VMEM((many1, 1, A), F32),
                pltpu.VMEM((many2, 1, A), F32),
                pltpu.VMEM((1, 1, A), F32),
                pltpu.VMEM((1, 1, A), F32),
                pltpu.SemaphoreType.DMA((4, 4)),
                pltpu.SemaphoreType.DMA((4, 4)),
                pltpu.SemaphoreType.DMA((2,)),
                pltpu.SemaphoreType.DMA((2,)),
            ],
            compiler_params=pltpu.CompilerParams(
                collective_id=0, has_side_effects=True, vmem_limit_bytes=56 * 1024 * 1024
            ),
            name="step",
        )(*arrays)
        return (outs[0].reshape(A),) + tuple(outs[1:])

    tail = P(None, ("slab", "sub"))
    flat = P(("slab", "sub"))
    placed = (tail, tail, flat, flat, tail, tail, P(None, None, ("slab", "sub")), tail, tail, tail) + (P(),) * 16
    return jax.shard_map(
        body,
        mesh=mesh,
        in_specs=placed,
        out_specs=(flat, tail, tail, tail, tail, P(), P()),
        check_vma=False,
    )
```

```python
import functools
import math

import jax
import jax.numpy as jnp
from jax import lax
from jax.experimental import pallas as pl
from jax.experimental.pallas import tpu as pltpu
from jax.sharding import PartitionSpec as P

MESH = pl.DeviceIdType.MESH
F32 = jnp.float32
BF16 = jnp.bfloat16
HIGHEST = lax.Precision.HIGHEST

cutoff = 5.0
neighbor_norm = 0.125
time_step = 0.5
outside_pressure = 0.5
box_mass = 0.125

C = 128
A = 128
K = 20
GH = 48
EXT = A + 4 * GH
CH = 4
NCH = K // CH
W = CH * A
E = K * A
RH = 64
LO = 2


def split2(x):
    high = x.astype(BF16)
    return high, (x - high.astype(F32)).astype(BF16)


def split3(x):
    high = x.astype(BF16).astype(F32)
    rest = x - high
    middle = rest.astype(BF16).astype(F32)
    return high, middle, rest - middle


def stack_left(weights):
    high, low = split2(weights)
    return jnp.concatenate([high, high, low], axis=1)


def stack_right(values):
    high, low = split2(values)
    return jnp.concatenate([high, low, high], axis=0)


def stack_basis(weights):
    h, m, l = split3(weights)
    return jnp.concatenate([h, h, h, m, m, l], axis=0).T.astype(BF16)


def stack_out(weights):
    high = weights.astype(BF16).astype(F32)
    return jnp.concatenate([high, high, weights - high], axis=0).T.astype(BF16)


def sine_cosine(turns):
    whole = jnp.floor(turns + 0.5)
    sign = 1.0 - 2.0 * (whole - 2.0 * jnp.floor(0.5 * whole))
    angle = (turns - whole) * math.pi
    square = angle * angle
    sine, cosine = jnp.zeros_like(square), jnp.zeros_like(square)
    for power in range(6, -1, -1):
        flip = (-1) ** power
        sine = sine * square + flip / math.factorial(2 * power + 1)
        cosine = cosine * square + flip / math.factorial(2 * power)
    return sine * angle * sign, cosine * sign


def mm(left, right):
    return jnp.dot(left, right, preferred_element_type=F32)


def mm_nt(left, right):
    return lax.dot_general(left, right, (((1,), (1,)), ((), ())), preferred_element_type=F32)


def mix(weights, values):
    return mm(stack_left(weights), stack_right(values))


def logistic(x):
    return 0.5 + 0.5 * jnp.tanh(0.5 * x)


def radial_net(start, win, mid0, mid1, out):
    pre = mm(win, start)
    for after in (mid0, mid1, out):
        half = pre.shape[1] // 2
        value, slope = pre[:, :half], pre[:, half:]
        gate = logistic(value)
        active = value * gate
        moved = (gate + active * (1.0 - gate)) * slope
        pre = mm(after, stack_right(jnp.concatenate([active, moved], axis=1)))
    return pre


def kernel(slabs, subs, *refs):
    (
        positions, velocities, species, ghost_species, neighbours, slot_mask, edges, send_slab, send_sub, migrants,
        embedding, energy_shift, masses, one_in, one_mid, one_out, node_one, two_in, two_mid, two_out, node_two,
        readout_linear, readout_hidden, readout_out, box_matrix, box_velocity,
        packed_out,
        lists, geo, element, basis, hot, kept1, slopes1, radial1, radial2, sums, pairs, table, parts, gather_parts,
        packed, gflat, send_a, recv_a, scat, recv_b, push, recv_c, send_d, recv_d, stage1, stage2,
        part1, part2, send_sem, recv_sem, sum_send, sum_recv,
    ) = refs
    slab, sub = lax.axis_index("slab"), lax.axis_index("sub")
    low, high = lax.rem(slab, LO), slab // LO
    many1, many2 = LO * subs, slabs // LO
    mine1 = low * subs + sub

    def first_peer(step):
        flat = lax.rem(mine1 + step, many1)
        return (high * LO + flat // subs, lax.rem(flat, subs))

    def second_peer(step):
        return (lax.rem(high + step, many2) * LO + low, sub)

    around = (
        (lax.rem(slab + slabs - 1, slabs), sub),
        (lax.rem(slab + 1, slabs), sub),
        (slab, lax.rem(sub + subs - 1, subs)),
        (slab, lax.rem(sub + 1, subs)),
    )
    barrier = pltpu.get_barrier_semaphore()

    def greet(device):
        pl.semaphore_signal(barrier, inc=1, device_id=device, device_id_type=MESH)

    for device in around:
        greet(device)

    @pl.loop(1, many1)
    def _(step):
        greet(first_peer(step))

    @pl.loop(1, many2)
    def _(step):
        greet(second_peer(step))

    def exchange(number, source, target):
        copies = []
        for block in (2, 3, 0, 1):
            copy = pltpu.make_async_remote_copy(
                src_ref=source(block),
                dst_ref=target(block ^ 1),
                send_sem=send_sem.at[number, block],
                recv_sem=recv_sem.at[number, block ^ 1],
                device_id=around[block],
                device_id_type=MESH,
            )
            copy.start()
            copies.append(copy)
        return copies

    def rows(block):
        return pl.ds(block * GH, GH)

    lane = lax.broadcasted_iota(jnp.int32, (1, A), 1)

    lists[...] = jnp.zeros_like(lists)
    lists[0:2, 0:GH] = send_slab[...].astype(F32)
    lists[2:4, 0:GH] = send_sub[...].astype(F32)
    lists[4:5, 0:16] = readout_out[...]
    lists[5:6, :] = readout_linear[...]
    columns = lists[...].T
    outer = jnp.broadcast_to(columns[:, 4:5], (C, A))
    linear = jnp.broadcast_to(columns[:, 5:6], (C, A))
    lanes_f = lax.broadcasted_iota(jnp.int32, (GH, A), 1).astype(F32)
    sent_f = jnp.concatenate(
        [(lanes_f == columns[0:GH, q : q + 1]).astype(F32) for q in range(4)], axis=0
    )
    sent_rows = sent_f.astype(BF16)
    sent_columns = sent_f.T.astype(BF16)

    ex, ey, ez = edges[0], edges[1], edges[2]
    distance = jnp.sqrt(ex * ex + ey * ey + ez * ez)
    inverse_distance = 1.0 / distance
    unit = (ex / distance, ey / distance, ez / distance)
    weight = slot_mask[...].astype(F32) * neighbor_norm
    for row, values in enumerate(unit + (weight, distance, inverse_distance)):
        for k in range(K):
            geo[row : row + 1, k * A : (k + 1) * A] = values[k : k + 1, :]

    kinds = lax.broadcasted_iota(jnp.int32, (8, A), 0)
    own_kind = (kinds == species[...]).astype(F32)
    pad8 = jnp.zeros((8, A), F32)
    near = neighbours[...]
    spot, group = near & (A - 1), near >> 7

    def look_up(row):
        spread = jnp.broadcast_to(row, (K, A))
        return jnp.take_along_axis(spread, spot, axis=1, mode="promise_in_bounds")

    ghosts = ghost_species[...]
    tail = jnp.concatenate([ghosts[:, A:], jnp.zeros((1, 2 * A - 4 * GH), jnp.int32)], axis=1)
    element[...] = jnp.where(
        group == 0, look_up(species[...]), jnp.where(group == 1, look_up(ghosts[:, 0:A]), look_up(tail))
    )

    orders = (lax.broadcasted_iota(jnp.int32, (8, 1), 0) + 1).astype(F32)
    scale = jnp.sqrt(2.0 / cutoff).astype(F32)

    one_in_s = stack_basis(one_in[...])
    one_mid0, one_mid1 = stack_left(one_mid[0]), stack_left(one_mid[1])
    one_out_s = stack_out(one_out[...])

    lifted = lax.dot_general(
        embedding[...], node_one[0], (((1,), (1,)), ((), ())), precision=HIGHEST, preferred_element_type=F32
    )
    lifted_s = jnp.concatenate(list(split3(lifted)) + [pad8], axis=0).T.astype(BF16)

    sums[...] = jnp.zeros_like(sums)

    def lanes_of(chunk):
        return pl.ds(pl.multiple_of(chunk * W, W), W)

    def first_forward(chunk, _):
        here = lanes_of(chunk)
        d = geo[4:5, here]
        inverse_d = geo[5:6, here]
        x = d / cutoff
        x2 = x * x
        x3 = x2 * x
        x5 = x2 * x3
        x6 = x3 * x3
        envelope = 1.0 - 28.0 * x6 + 48.0 * x6 * x - 21.0 * x6 * x2
        slope = (-168.0 * x5 + 336.0 * x6 - 168.0 * x6 * x) / cutoff
        sine, cosine = sine_cosine(orders * x)
        even = scale * inverse_d * envelope
        values = sine * even
        slopes = cosine * (orders * (math.pi / cutoff)) * even + sine * (
            scale * inverse_d * (slope - envelope * inverse_d)
        )
        h, m, l = split3(jnp.concatenate([values, slopes], axis=1))
        start = jnp.concatenate([h, m, l, h, m, h], axis=0).astype(BF16)
        basis[chunk] = start
        pre = mm(one_in_s, start[:, 0:W])
        for layer, after in enumerate((one_mid0, one_mid1, one_out_s)):
            gate = logistic(pre)
            active = pre * gate
            slopes1[chunk, layer * RH : (layer + 1) * RH] = gate + active * (1.0 - gate)
            pre = mm(after, stack_right(active))
        radial1[...] = pre
        kind8 = jnp.concatenate(
            [(kinds == element[pl.ds(chunk * CH + j, 1), :]).astype(F32) for j in range(CH)], axis=1
        )
        picked_x = mm(lifted_s, jnp.concatenate([kind8, kind8, kind8, jnp.zeros_like(kind8)], axis=0).astype(BF16))
        total = [jnp.zeros((C, A), F32) for _ in range(4)]
        for j in range(CH):
            cut = slice(j * A, (j + 1) * A)
            at = pl.ds(pl.multiple_of(chunk * W + j * A, A), A)
            wx = picked_x[:, cut] * geo[3:4, at]
            total[0] += radial1[0:C, cut] * wx
            q1 = radial1[C : 2 * C, cut] * wx
            for a in range(3):
                total[a + 1] += geo[a : a + 1, at] * q1
            kept1[chunk, 0:C, cut] = q1
            kept1[chunk, C : 2 * C, cut] = wx
        for a in range(4):
            sums[a] += total[a]
        return 0

    def first_slopes(chunk, _):
        pre = mm(one_in_s, basis[chunk, :, W : 2 * W])
        for layer, after in enumerate((one_mid0, one_mid1, one_out_s)):
            pre = mm(after, stack_right(slopes1[chunk, layer * RH : (layer + 1) * RH] * pre))
        wx = kept1[chunk, C : 2 * C]
        kept1[chunk, C : 2 * C] = pre[0:C] * wx
        kept1[chunk, 2 * C : 3 * C] = pre[C : 2 * C] * wx
        return 0

    lax.fori_loop(0, NCH, first_forward, 0, unroll=True)

    s0 = mm(
        jnp.concatenate(list(split3(embedding[...])) + [pad8], axis=0).T.astype(BF16),
        jnp.concatenate([own_kind, own_kind, own_kind, pad8], axis=0).astype(BF16),
    )
    a0 = sums[0]
    a1 = [sums[1], sums[2], sums[3]]
    square = a1[0] * a1[0] + a1[1] * a1[1] + a1[2] * a1[2]
    s1 = s0 + mix(node_one[1], a0) + mix(node_one[2], a0 * a0) + mix(node_one[3], square)
    turned = mix(node_one[4], jnp.concatenate(a1, axis=1))
    gate1 = mix(node_one[5], a0)
    v1 = jnp.concatenate([turned[:, a * A : (a + 1) * A] + gate1 * a1[a] for a in range(3)], axis=1)
    lifted_x = mix(node_two[0], s1)
    lifted_y = mix(node_two[1], v1)
    own_table = jnp.concatenate([lifted_x] + [lifted_y[:, a * A : (a + 1) * A] for a in range(3)], axis=0)
    own_high, own_low = split2(own_table)
    send_a[...] = mm_nt(sent_rows, own_high) + mm_nt(sent_rows, own_low)
    table[:, 0:A] = own_high
    table[:, A : 2 * A] = own_low

    pl.semaphore_wait(barrier, 4 + many1 - 1 + many2 - 1)
    copies_a = exchange(0, lambda q: send_a.at[rows(q)], lambda q: recv_a.at[rows(q)])

    two_in_s = stack_basis(two_in[...])
    two_mid0, two_mid1 = stack_left(two_mid[0]), stack_left(two_mid[1])
    two_out_s = stack_out(two_out[...])

    def second_radial(chunk, _):
        row_of = lax.broadcasted_iota(jnp.int32, (EXT, A), 0)
        for j in range(CH):
            picked = neighbours[pl.ds(chunk * CH + j, 1), :]
            hot[chunk, :, j * A : (j + 1) * A] = (row_of == picked).astype(F32).astype(BF16)
        radial2[chunk] = radial_net(basis[chunk], two_in_s, two_mid0, two_mid1, two_out_s)
        own_hot = hot[chunk, 0:A, :]
        pairs[chunk] = mm(table[...], jnp.concatenate([own_hot, own_hot], axis=0))
        return 0

    lax.fori_loop(0, NCH, second_radial, 0, unroll=True)

    for copy in copies_a:
        copy.wait_recv()
    ghost_high, ghost_low = split2(recv_a[...].T)
    gather_parts[:, 0 : 4 * GH] = ghost_high
    gather_parts[:, 4 * GH : 8 * GH] = ghost_low

    sums2 = parts
    sums2[...] = jnp.zeros_like(sums2)

    def second_forward(chunk, _):
        far_hot = hot[chunk, A:EXT, :]
        pairs[chunk] += mm(gather_parts[...], jnp.concatenate([far_hot, far_hot], axis=0))
        total = [jnp.zeros((C, A), F32) for _ in range(4)]
        for j in range(CH):
            cut = slice(j * A, (j + 1) * A)
            at = pl.ds(pl.multiple_of(chunk * W + j * A, A), A)
            w = geo[3:4, at]
            u = [geo[a : a + 1, at] for a in range(3)]
            wx = pairs[chunk, 0:C, cut] * w
            wy = [pairs[chunk, (a + 1) * C : (a + 2) * C, cut] * w for a in range(3)]
            along = wy[0] * u[0] + wy[1] * u[1] + wy[2] * u[2]
            total[0] += radial2[chunk, 0:C, cut] * wx + radial2[chunk, 3 * C : 4 * C, cut] * along
            r1x = radial2[chunk, C : 2 * C, cut] * wx
            r2 = radial2[chunk, 2 * C : 3 * C, cut]
            for a in range(3):
                total[a + 1] += r1x * u[a] + r2 * wy[a]
        for a in range(4):
            sums2[a] += total[a]
        return 0

    lax.fori_loop(0, NCH, second_forward, 0)

    b0 = sums2[0]
    b1 = [sums2[1], sums2[2], sums2[3]]
    square2 = b1[0] * b1[0] + b1[1] * b1[1] + b1[2] * b1[2]
    s2 = s1 + mix(node_two[2], b0) + mix(node_two[3], b0 * b0) + mix(node_two[4], square2)
    inner = jnp.concatenate([readout_hidden[...], jnp.zeros((C - 16, C), F32)], axis=0)
    pre = mix(inner, s2)
    gate2 = logistic(pre)
    hidden = pre * gate2
    shift = jnp.zeros((1, A), F32)
    mass = jnp.zeros((1, A), F32)
    for s in range(8):
        shift = jnp.where(species[...] == s, energy_shift[s], shift)
        mass = jnp.where(species[...] == s, masses[s], mass)
    packed_out[0:1, :] = (
        shift + jnp.sum(linear * s1, axis=0, keepdims=True) + jnp.sum(outer * hidden, axis=0, keepdims=True)
    )
    back_pre = outer * (gate2 + hidden * (1.0 - gate2))
    back_s2 = mix(inner.T, back_pre)
    back_b0 = mix(node_two[2].T, back_s2) + 2.0 * b0 * mix(node_two[3].T, back_s2)
    back_square2 = 2.0 * mix(node_two[4].T, back_s2)
    sums2[0] = back_b0
    for a in range(3):
        sums2[a + 1] = b1[a] * back_square2

    scat[...] = jnp.zeros_like(scat)

    def second_back(side, chunk, _):
        for j in range(CH):
            cut = slice(j * A, (j + 1) * A)
            far = slice(W + j * A, W + (j + 1) * A)
            at = pl.ds(pl.multiple_of(chunk * W + j * A, A), A)
            w = geo[3:4, at]
            wu = [w * geo[a : a + 1, at] for a in range(3)]
            r3 = radial2[chunk, 3 * C : 4 * C, cut]
            r2 = radial2[chunk, 2 * C : 3 * C, cut]

            def vector_part(a):
                return r3 * (sums2[0] * wu[a]) + r2 * (sums2[a + 1] * w)

            if side == 0:
                dot_u = sums2[1] * wu[0] + sums2[2] * wu[1] + sums2[3] * wu[2]
                back = [
                    radial2[chunk, 0:C, cut] * (sums2[0] * w) + radial2[chunk, C : 2 * C, cut] * dot_u,
                    vector_part(0),
                ]
            else:
                back = [vector_part(1), vector_part(2)]
            for a in range(2):
                h, l = split2(back[a])
                kept = slice(a * C, (a + 1) * C)
                packed[kept, cut] = h
                packed[kept, far] = l
        hot_here = hot[chunk]
        half = slice(side * 2 * C, (side + 1) * 2 * C)
        scat[:, half] += mm_nt(hot_here, packed[:, 0:W]) + mm_nt(hot_here, packed[:, W : 2 * W])
        return 0

    copies_b = []
    for side in range(2):
        lax.fori_loop(0, NCH, functools.partial(second_back, side), 0)
        half = pl.ds(side * 2 * C, 2 * C)
        copies_b += exchange(
            1 + side, lambda q: scat.at[pl.ds(A + q * GH, GH), half], lambda q: recv_b.at[rows(q), half]
        )

    def second_edges(chunk, _):
        for j in range(CH):
            cut = slice(j * A, (j + 1) * A)
            far = slice(W + j * A, W + (j + 1) * A)
            at = pl.ds(pl.multiple_of(chunk * W + j * A, A), A)
            w = geo[3:4, at]
            u = [geo[a : a + 1, at] for a in range(3)]
            k0 = sums2[0]
            k1 = [sums2[a + 1] for a in range(3)]
            x = pairs[chunk, 0:C, cut]
            y = [pairs[chunk, (a + 1) * C : (a + 2) * C, cut] for a in range(3)]
            dot_u = k1[0] * u[0] + k1[1] * u[1] + k1[2] * u[2]
            along = y[0] * u[0] + y[1] * u[1] + y[2] * u[2]
            cross = y[0] * k1[0] + y[1] * k1[1] + y[2] * k1[2]
            stretch = (
                (radial2[chunk, 0:C, far] * k0 + radial2[chunk, C : 2 * C, far] * dot_u) * x
                + radial2[chunk, 3 * C : 4 * C, far] * along * k0
                + radial2[chunk, 2 * C : 3 * C, far] * cross
            )
            gflat[3:4, at] = w * jnp.sum(stretch, axis=0, keepdims=True)
            r3k0 = radial2[chunk, 3 * C : 4 * C, cut] * k0
            r1x = radial2[chunk, C : 2 * C, cut] * x
            for a in range(3):
                gflat[a : a + 1, at] = w * jnp.sum(r3k0 * y[a] + r1x * k1[a], axis=0, keepdims=True)
        return 0

    lax.fori_loop(0, NCH, second_edges, 0)
    lax.fori_loop(0, NCH, first_slopes, 0, unroll=True)

    for copy in copies_b:
        copy.wait_recv()
    back_high, back_low = split2(recv_b[...])
    back_table = (scat[0:A] + mm(sent_columns, back_high) + mm(sent_columns, back_low)).T
    back_s1 = back_s2 + linear + mix(node_two[0].T, back_table[0:C])
    back_v1 = mix(
        node_two[1].T, jnp.concatenate([back_table[(a + 1) * C : (a + 2) * C] for a in range(3)], axis=1)
    )
    back_turned = mix(node_one[4].T, back_v1)
    back_square = 2.0 * mix(node_one[3].T, back_s1)
    cut_v = [back_v1[:, a * A : (a + 1) * A] for a in range(3)]
    back_gate = a1[0] * cut_v[0] + a1[1] * cut_v[1] + a1[2] * cut_v[2]
    sums[0] = (
        mix(node_one[1].T, back_s1) + 2.0 * a0 * mix(node_one[2].T, back_s1) + mix(node_one[5].T, back_gate)
    )
    for a in range(3):
        sums[a + 1] = back_turned[:, a * A : (a + 1) * A] + gate1 * cut_v[a] + a1[a] * back_square

    push[...] = jnp.zeros_like(push)

    def first_edges(chunk, _):
        pieces = []
        for j in range(CH):
            cut = slice(j * A, (j + 1) * A)
            at = pl.ds(pl.multiple_of(chunk * W + j * A, A), A)
            u = [geo[a : a + 1, at] for a in range(3)]
            inverse_d = geo[5:6, at]
            k1 = [sums[a + 1] for a in range(3)]
            q1 = kept1[chunk, 0:C, cut]
            dot_u = k1[0] * u[0] + k1[1] * u[1] + k1[2] * u[2]
            stretch = gflat[3:4, at] + jnp.sum(
                kept1[chunk, C : 2 * C, cut] * sums[0] + kept1[chunk, 2 * C : 3 * C, cut] * dot_u,
                axis=0,
                keepdims=True,
            )
            turn = [gflat[a : a + 1, at] + jnp.sum(q1 * k1[a], axis=0, keepdims=True) for a in range(3)]
            inward = turn[0] * u[0] + turn[1] * u[1] + turn[2] * u[2]
            radial_part = stretch - inward * inverse_d
            for a in range(3):
                gflat[a : a + 1, at] = radial_part * u[a] + turn[a] * inverse_d
            gflat[3:8, at] = jnp.zeros((5, A), F32)
        g = gflat[:, lanes_of(chunk)]
        g_high = g.astype(BF16).astype(F32)
        both = jnp.concatenate([g_high, g - g_high], axis=0).astype(BF16)
        push[...] += mm_nt(hot[chunk], both)
        return 0

    lax.fori_loop(0, NCH, first_edges, 0)
    pushed = push[...]
    pushed = pushed[:, 0:8] + pushed[:, 8:16]
    push[:, 0:8] = pushed
    copies_c = exchange(3, lambda q: push.at[pl.ds(A + q * GH, GH)], lambda q: recv_c.at[rows(q)])

    own = jnp.zeros((8, A), F32)
    virial = [[jnp.zeros((1, A), F32) for _ in range(3)] for _ in range(3)]
    for k in range(K):
        own += gflat[:, k * A : (k + 1) * A]
        for a in range(3):
            for b in range(3):
                virial[a][b] += edges[a, k : k + 1, :] * gflat[b : b + 1, k * A : (k + 1) * A]
    for copy in copies_c:
        copy.wait_recv()
    come_high, come_low = split2(recv_c[...])
    back_f = (push[0:A] + mm(sent_columns, come_high) + mm(sent_columns, come_low)).T
    forces = own[0:3] - back_f[0:3]
    packed_out[8:11, :] = forces
    new_velocities = velocities[...] + time_step * forces / mass
    packed_out[16:19, :] = new_velocities

    order = (1, 0, 3, 2)
    movers = jnp.full((1, A), -1, jnp.int32)
    for q in range(4):
        for j in range(4):
            movers = jnp.where(lane == 4 * q + j, migrants[order[q], j], movers)
    chosen = (lax.broadcasted_iota(jnp.int32, (A, A), 0) == movers).astype(F32).astype(BF16)
    state = jnp.concatenate([positions[...], new_velocities, jnp.zeros((2, A), F32)], axis=0)
    h, m, l = split3(state)
    sent_state = mm(jnp.concatenate([h, m, l, jnp.zeros_like(h)], axis=0).astype(BF16), chosen)
    send_d[...] = sent_state[0:8] + sent_state[8:16] + sent_state[16:24]
    copies_d = exchange(4, lambda q: send_d, lambda q: recv_d.at[q])

    mine = jnp.zeros((1, A), F32)
    for a in range(3):
        for b in range(3):
            term = new_velocities[a : a + 1] * mass * new_velocities[b : b + 1] - virial[a][b]
            mine = jnp.where(lane == 3 * a + b, jnp.sum(term, axis=1, keepdims=True), mine)

    def all_sum(number, value, part, stage, many, me, peer):
        part[...] = value.reshape(1, 1, A)
        stage[pl.ds(me, 1)] = value.reshape(1, 1, A)

        @pl.loop(1, many)
        def _(step):
            pltpu.make_async_remote_copy(
                src_ref=part,
                dst_ref=stage.at[pl.ds(me, 1)],
                send_sem=sum_send.at[number],
                recv_sem=sum_recv.at[number],
                device_id=peer(step),
                device_id_type=MESH,
            ).start()

        whole = stage.at[pl.ds(0, many - 1)]
        pltpu.make_async_copy(whole, whole, sum_recv.at[number]).wait()
        pltpu.make_async_copy(whole, whole, sum_send.at[number]).wait()
        return jnp.sum(stage[...], axis=0)

    near = all_sum(0, mine, part1, stage1, many1, mine1, first_peer)
    stress_row = all_sum(1, near, part2, stage2, many2, high, second_peer)

    def entry(ref, a, b):
        return jnp.full((1, A), ref[a, b], F32)

    def determinant(m):
        return (
            m[0][0] * (m[1][1] * m[2][2] - m[1][2] * m[2][1])
            - m[0][1] * (m[1][0] * m[2][2] - m[1][2] * m[2][0])
            + m[0][2] * (m[1][0] * m[2][1] - m[1][1] * m[2][0])
        )

    def inverse(m):
        det = determinant(m)
        cof = [
            [
                m[(r + 1) % 3][(c + 1) % 3] * m[(r + 2) % 3][(c + 2) % 3]
                - m[(r + 1) % 3][(c + 2) % 3] * m[(r + 2) % 3][(c + 1) % 3]
                for c in range(3)
            ]
            for r in range(3)
        ]
        return [[cof[c][r] / det for c in range(3)] for r in range(3)]

    box = [[entry(box_matrix, a, b) for b in range(3)] for a in range(3)]
    volume = determinant(box)
    inv = inverse(box)
    total_atoms = box_mass * (A * slabs * subs)
    pressed = []
    for a in range(3):
        line = []
        for b in range(3):
            value = jnp.broadcast_to(stress_row[:, 3 * a + b : 3 * a + b + 1], (1, A))
            line.append(value - outside_pressure * volume if a == b else value)
        pressed.append(line)
    box_speed = []
    for a in range(3):
        line = []
        for b in range(3):
            pushed_box = pressed[a][0] * inv[b][0] + pressed[a][1] * inv[b][1] + pressed[a][2] * inv[b][2]
            line.append(entry(box_velocity, a, b) + time_step * pushed_box / total_atoms)
        box_speed.append(line)
    new_box = [[box[a][b] + time_step * box_speed[a][b] for b in range(3)] for a in range(3)]
    new_inverse = inverse(new_box)
    for group_at, matrix in ((40, new_box), (48, box_speed)):
        for a in range(3):
            line = jnp.where(lane == 0, matrix[a][0], jnp.where(lane == 1, matrix[a][1], matrix[a][2]))
            packed_out[group_at + a : group_at + a + 1, :] = line

    def drift(moving):
        return [
            new_inverse[a][0] * moving[0:1] + new_inverse[a][1] * moving[1:2] + new_inverse[a][2] * moving[2:3]
            for a in range(3)
        ]

    moved = drift(new_velocities)
    for a in range(3):
        packed_out[24 + a : 25 + a, :] = positions[a : a + 1, :] + time_step * moved[a]
    for copy in copies_d:
        copy.wait_recv()
    come = jnp.where(
        lane < 4, recv_d[0], jnp.where(lane < 8, recv_d[1], jnp.where(lane < 12, recv_d[2], recv_d[3]))
    )
    moved = drift(come[3:6])
    for a in range(3):
        packed_out[32 + a : 33 + a, :] = come[a : a + 1] + time_step * moved[a]
    packed_out[35:38, :] = come[3:6]

    for copies in (copies_a, copies_b, copies_c, copies_d):
        for copy in copies:
            copy.wait_send()


def unpack(held, *outs):
    for i, out in enumerate(outs):
        out[...] = held[8 * i : 8 * i + out.shape[0], 0 : out.shape[1]]


def solution(mesh):
    slabs, subs = mesh.shape["slab"], mesh.shape["sub"]
    many1, many2 = LO * subs, slabs // LO
    vmem = pl.BlockSpec(memory_space=pltpu.VMEM)
    smem = pl.BlockSpec(memory_space=pltpu.SMEM)
    in_smem = {9, 11, 12, 24, 25}

    def body(*arrays):
        arrays = list(arrays)
        for position in (2, 3, 21, 23):
            arrays[position] = arrays[position].reshape(1, -1)
        for position in (13, 15, 17, 19):
            arrays[position] = arrays[position].T
        shapes = [(1, A), (3, A), (3, A), (3, A), (6, 16), (3, 3), (3, 3)]
        held = pl.pallas_call(
            functools.partial(kernel, slabs, subs),
            out_shape=jax.ShapeDtypeStruct((8 * len(shapes), A), F32),
            in_specs=[smem if i in in_smem else vmem for i in range(26)],
            out_specs=vmem,
            scratch_shapes=[
                pltpu.VMEM((8, 128), F32),
                pltpu.VMEM((8, E), F32),
                pltpu.VMEM((K, A), jnp.int32),
                pltpu.VMEM((NCH, 48, 2 * W), BF16),
                pltpu.VMEM((NCH, EXT, W), BF16),
                pltpu.VMEM((NCH, 3 * C, W), F32),
                pltpu.VMEM((NCH, 3 * RH, W), F32),
                pltpu.VMEM((2 * C, W), F32),
                pltpu.VMEM((NCH, 4 * C, 2 * W), F32),
                pltpu.VMEM((4, C, A), F32),
                pltpu.VMEM((NCH, 4 * C, W), F32),
                pltpu.VMEM((4 * C, 2 * A), BF16),
                pltpu.VMEM((4, C, A), F32),
                pltpu.VMEM((4 * C, 8 * GH), BF16),
                pltpu.VMEM((2 * C, 2 * W), BF16),
                pltpu.VMEM((8, E), F32),
                pltpu.VMEM((4 * GH, 4 * C), F32),
                pltpu.VMEM((4 * GH, 4 * C), F32),
                pltpu.VMEM((EXT, 4 * C), F32),
                pltpu.VMEM((4 * GH, 4 * C), F32),
                pltpu.VMEM((EXT, 16), F32),
                pltpu.VMEM((4 * GH, 16), F32),
                pltpu.VMEM((8, A), F32),
                pltpu.VMEM((4, 8, A), F32),
                pltpu.VMEM((many1, 1, A), F32),
                pltpu.VMEM((many2, 1, A), F32),
                pltpu.VMEM((1, 1, A), F32),
                pltpu.VMEM((1, 1, A), F32),
                pltpu.SemaphoreType.DMA((5, 4)),
                pltpu.SemaphoreType.DMA((5, 4)),
                pltpu.SemaphoreType.DMA((2,)),
                pltpu.SemaphoreType.DMA((2,)),
            ],
            compiler_params=pltpu.CompilerParams(
                collective_id=0, has_side_effects=True, vmem_limit_bytes=56 * 1024 * 1024
            ),
            name="step",
        )(*arrays)
        outs = pl.pallas_call(
            unpack,
            out_shape=[jax.ShapeDtypeStruct(shape, F32) for shape in shapes],
            in_specs=[vmem],
            out_specs=[vmem] * 7,
            name="unpack",
        )(held)
        return (outs[0].reshape(A),) + tuple(outs[1:])

    tail = P(None, ("slab", "sub"))
    flat = P(("slab", "sub"))
    placed = (tail, tail, flat, flat, tail, tail, P(None, None, ("slab", "sub")), tail, tail, tail) + (P(),) * 16
    return jax.shard_map(
        body,
        mesh=mesh,
        in_specs=placed,
        out_specs=(flat, tail, tail, tail, tail, P(), P()),
        check_vma=False,
    )
```

```python
import functools
import math

import jax
import jax.numpy as jnp
from jax import lax
from jax.experimental import pallas as pl
from jax.experimental.pallas import tpu as pltpu
from jax.sharding import PartitionSpec as P

MESH = pl.DeviceIdType.MESH
F32 = jnp.float32
BF16 = jnp.bfloat16
HIGHEST = lax.Precision.HIGHEST

cutoff = 5.0
neighbor_norm = 0.125
time_step = 0.5
outside_pressure = 0.5
box_mass = 0.125

C = 128
A = 128
K = 20
GH = 48
EXT = A + 4 * GH
CH = 4
NCH = K // CH
W = CH * A
E = K * A
RH = 64
LO = 2


def split2(x):
    high = x.astype(BF16)
    return high, (x - high.astype(F32)).astype(BF16)


def split3(x):
    high = x.astype(BF16).astype(F32)
    rest = x - high
    middle = rest.astype(BF16).astype(F32)
    return high, middle, rest - middle


def stack_left(weights):
    high, low = split2(weights)
    return jnp.concatenate([high, high, low], axis=1)


def stack_right(values):
    high, low = split2(values)
    return jnp.concatenate([high, low, high], axis=0)


def stack_basis(weights):
    h, m, l = split3(weights)
    return jnp.concatenate([h, h, h, m, m, l], axis=0).T.astype(BF16)


def stack_out(weights):
    high = weights.astype(BF16).astype(F32)
    return jnp.concatenate([high, high, weights - high], axis=0).T.astype(BF16)


def sine_cosine(turns):
    whole = jnp.floor(turns + 0.5)
    sign = 1.0 - 2.0 * (whole - 2.0 * jnp.floor(0.5 * whole))
    angle = (turns - whole) * math.pi
    square = angle * angle
    sine, cosine = jnp.zeros_like(square), jnp.zeros_like(square)
    for power in range(6, -1, -1):
        flip = (-1) ** power
        sine = sine * square + flip / math.factorial(2 * power + 1)
        cosine = cosine * square + flip / math.factorial(2 * power)
    return sine * angle * sign, cosine * sign


def mm(left, right):
    return jnp.dot(left, right, preferred_element_type=F32)


def mm_nt(left, right):
    return lax.dot_general(left, right, (((1,), (1,)), ((), ())), preferred_element_type=F32)


def mix(weights, values):
    return mm(stack_left(weights), stack_right(values))


def logistic(x):
    return 0.5 + 0.5 * jnp.tanh(0.5 * x)


def radial_net(start, win, mid0, mid1, out):
    pre = mm(win, start)
    for after in (mid0, mid1, out):
        half = pre.shape[1] // 2
        value, slope = pre[:, :half], pre[:, half:]
        gate = logistic(value)
        active = value * gate
        moved = (gate + active * (1.0 - gate)) * slope
        pre = mm(after, stack_right(jnp.concatenate([active, moved], axis=1)))
    return pre


def kernel(slabs, subs, *refs):
    (
        positions, velocities, species, ghost_species, neighbours, slot_mask, edges, send_slab, send_sub, migrants,
        embedding, energy_shift, masses, one_in, one_mid, one_out, node_one, two_in, two_mid, two_out, node_two,
        readout_linear, readout_hidden, readout_out, box_matrix, box_velocity,
        packed_out,
        lists, geo, element, basis, hot, kept1, slopes1, radial1, radial2, sums, pairs, table, parts, gather_parts,
        packed, gflat, send_a, recv_a, scat, recv_b, push, recv_c, send_d, recv_d, stage1, stage2,
        part1, part2, send_sem, recv_sem, sum_send, sum_recv,
    ) = refs
    slab, sub = lax.axis_index("slab"), lax.axis_index("sub")
    low, high = lax.rem(slab, LO), slab // LO
    many1, many2 = LO * subs, slabs // LO
    mine1 = low * subs + sub

    def first_peer(step):
        flat = lax.rem(mine1 + step, many1)
        return (high * LO + flat // subs, lax.rem(flat, subs))

    def second_peer(step):
        return (lax.rem(high + step, many2) * LO + low, sub)

    around = (
        (lax.rem(slab + slabs - 1, slabs), sub),
        (lax.rem(slab + 1, slabs), sub),
        (slab, lax.rem(sub + subs - 1, subs)),
        (slab, lax.rem(sub + 1, subs)),
    )
    barrier = pltpu.get_barrier_semaphore()

    def greet(device):
        pl.semaphore_signal(barrier, inc=1, device_id=device, device_id_type=MESH)

    for device in around:
        greet(device)

    @pl.loop(1, many1)
    def _(step):
        greet(first_peer(step))

    @pl.loop(1, many2)
    def _(step):
        greet(second_peer(step))

    def exchange(number, source, target):
        copies = []
        for block in (2, 3, 0, 1):
            copy = pltpu.make_async_remote_copy(
                src_ref=source(block),
                dst_ref=target(block ^ 1),
                send_sem=send_sem.at[number, block],
                recv_sem=recv_sem.at[number, block ^ 1],
                device_id=around[block],
                device_id_type=MESH,
            )
            copy.start()
            copies.append(copy)
        return copies

    def rows(block):
        return pl.ds(block * GH, GH)

    lane = lax.broadcasted_iota(jnp.int32, (1, A), 1)

    lists[...] = jnp.zeros_like(lists)
    lists[0:2, 0:GH] = send_slab[...].astype(F32)
    lists[2:4, 0:GH] = send_sub[...].astype(F32)
    lists[4:5, 0:16] = readout_out[...]
    lists[5:6, :] = readout_linear[...]
    columns = lists[...].T
    outer = jnp.broadcast_to(columns[:, 4:5], (C, A))
    linear = jnp.broadcast_to(columns[:, 5:6], (C, A))
    lanes_f = lax.broadcasted_iota(jnp.int32, (GH, A), 1).astype(F32)
    sent_f = jnp.concatenate(
        [(lanes_f == columns[0:GH, q : q + 1]).astype(F32) for q in range(4)], axis=0
    )
    sent_rows = sent_f.astype(BF16)
    sent_columns = sent_f.T.astype(BF16)

    ex, ey, ez = edges[0], edges[1], edges[2]
    distance = jnp.sqrt(ex * ex + ey * ey + ez * ez)
    inverse_distance = 1.0 / distance
    unit = (ex / distance, ey / distance, ez / distance)
    weight = slot_mask[...].astype(F32) * neighbor_norm
    for row, values in enumerate(unit + (weight, distance, inverse_distance)):
        for k in range(K):
            geo[row : row + 1, k * A : (k + 1) * A] = values[k : k + 1, :]

    kinds = lax.broadcasted_iota(jnp.int32, (8, A), 0)
    own_kind = (kinds == species[...]).astype(F32)
    pad8 = jnp.zeros((8, A), F32)
    near = neighbours[...]
    spot, group = near & (A - 1), near >> 7

    def look_up(row):
        spread = jnp.broadcast_to(row, (K, A))
        return jnp.take_along_axis(spread, spot, axis=1, mode="promise_in_bounds")

    ghosts = ghost_species[...]
    tail = jnp.concatenate([ghosts[:, A:], jnp.zeros((1, 2 * A - 4 * GH), jnp.int32)], axis=1)
    element[...] = jnp.where(
        group == 0, look_up(species[...]), jnp.where(group == 1, look_up(ghosts[:, 0:A]), look_up(tail))
    )

    orders = (lax.broadcasted_iota(jnp.int32, (8, 1), 0) + 1).astype(F32)
    scale = jnp.sqrt(2.0 / cutoff).astype(F32)

    one_in_s = stack_basis(one_in[...])
    one_mid0, one_mid1 = stack_left(one_mid[0]), stack_left(one_mid[1])
    one_out_s = stack_out(one_out[...])

    lifted = lax.dot_general(
        embedding[...], node_one[0], (((1,), (1,)), ((), ())), precision=HIGHEST, preferred_element_type=F32
    )
    lifted_s = jnp.concatenate(list(split3(lifted)) + [pad8], axis=0).T.astype(BF16)

    sums[...] = jnp.zeros_like(sums)

    def lanes_of(chunk):
        return pl.ds(pl.multiple_of(chunk * W, W), W)

    def first_forward(chunk, _):
        here = lanes_of(chunk)
        d = geo[4:5, here]
        inverse_d = geo[5:6, here]
        x = d / cutoff
        x2 = x * x
        x3 = x2 * x
        x5 = x2 * x3
        x6 = x3 * x3
        envelope = 1.0 - 28.0 * x6 + 48.0 * x6 * x - 21.0 * x6 * x2
        slope = (-168.0 * x5 + 336.0 * x6 - 168.0 * x6 * x) / cutoff
        sine, cosine = sine_cosine(orders * x)
        even = scale * inverse_d * envelope
        values = sine * even
        slopes = cosine * (orders * (math.pi / cutoff)) * even + sine * (
            scale * inverse_d * (slope - envelope * inverse_d)
        )
        h, m, l = split3(jnp.concatenate([values, slopes], axis=1))
        start = jnp.concatenate([h, m, l, h, m, h], axis=0).astype(BF16)
        basis[chunk] = start
        pre = mm(one_in_s, start[:, 0:W])
        for layer, after in enumerate((one_mid0, one_mid1, one_out_s)):
            gate = logistic(pre)
            active = pre * gate
            slopes1[chunk, layer * RH : (layer + 1) * RH] = gate + active * (1.0 - gate)
            pre = mm(after, stack_right(active))
        radial1[...] = pre
        kind8 = jnp.concatenate(
            [(kinds == element[pl.ds(chunk * CH + j, 1), :]).astype(F32) for j in range(CH)], axis=1
        )
        picked_x = mm(lifted_s, jnp.concatenate([kind8, kind8, kind8, jnp.zeros_like(kind8)], axis=0).astype(BF16))
        total = [jnp.zeros((C, A), F32) for _ in range(4)]
        for j in range(CH):
            cut = slice(j * A, (j + 1) * A)
            at = pl.ds(pl.multiple_of(chunk * W + j * A, A), A)
            wx = picked_x[:, cut] * geo[3:4, at]
            total[0] += radial1[0:C, cut] * wx
            q1 = radial1[C : 2 * C, cut] * wx
            for a in range(3):
                total[a + 1] += geo[a : a + 1, at] * q1
            kept1[chunk, 0:C, cut] = q1
            kept1[chunk, C : 2 * C, cut] = wx
        for a in range(4):
            sums[a] += total[a]
        return 0

    def first_slopes(chunk, _):
        pre = mm(one_in_s, basis[chunk, :, W : 2 * W])
        for layer, after in enumerate((one_mid0, one_mid1, one_out_s)):
            pre = mm(after, stack_right(slopes1[chunk, layer * RH : (layer + 1) * RH] * pre))
        wx = kept1[chunk, C : 2 * C]
        kept1[chunk, C : 2 * C] = pre[0:C] * wx
        kept1[chunk, 2 * C : 3 * C] = pre[C : 2 * C] * wx
        return 0

    lax.fori_loop(0, NCH, first_forward, 0, unroll=True)

    s0 = mm(
        jnp.concatenate(list(split3(embedding[...])) + [pad8], axis=0).T.astype(BF16),
        jnp.concatenate([own_kind, own_kind, own_kind, pad8], axis=0).astype(BF16),
    )
    a0 = sums[0]
    a1 = [sums[1], sums[2], sums[3]]
    square = a1[0] * a1[0] + a1[1] * a1[1] + a1[2] * a1[2]
    s1 = s0 + mix(node_one[1], a0) + mix(node_one[2], a0 * a0) + mix(node_one[3], square)
    turned = mix(node_one[4], jnp.concatenate(a1, axis=1))
    gate1 = mix(node_one[5], a0)
    v1 = jnp.concatenate([turned[:, a * A : (a + 1) * A] + gate1 * a1[a] for a in range(3)], axis=1)
    lifted_x = mix(node_two[0], s1)
    lifted_y = mix(node_two[1], v1)
    own_table = jnp.concatenate([lifted_x] + [lifted_y[:, a * A : (a + 1) * A] for a in range(3)], axis=0)
    own_high, own_low = split2(own_table)
    send_a[...] = mm_nt(sent_rows, own_high) + mm_nt(sent_rows, own_low)
    table[:, 0:A] = own_high
    table[:, A : 2 * A] = own_low

    pl.semaphore_wait(barrier, 4 + many1 - 1 + many2 - 1)
    copies_a = exchange(0, lambda q: send_a.at[rows(q)], lambda q: recv_a.at[rows(q)])

    two_in_s = stack_basis(two_in[...])
    two_mid0, two_mid1 = stack_left(two_mid[0]), stack_left(two_mid[1])
    two_out_s = stack_out(two_out[...])

    def second_radial(chunk, _):
        row_of = lax.broadcasted_iota(jnp.int32, (EXT, A), 0)
        for j in range(CH):
            picked = neighbours[pl.ds(chunk * CH + j, 1), :]
            hot[chunk, :, j * A : (j + 1) * A] = (row_of == picked).astype(F32).astype(BF16)
        radial2[chunk] = radial_net(basis[chunk], two_in_s, two_mid0, two_mid1, two_out_s)
        own_hot = hot[chunk, 0:A, :]
        pairs[chunk] = mm(table[...], jnp.concatenate([own_hot, own_hot], axis=0))
        return 0

    lax.fori_loop(0, NCH, second_radial, 0, unroll=True)
    lax.fori_loop(0, NCH, first_slopes, 0, unroll=True)

    for copy in copies_a:
        copy.wait_recv()
    ghost_high, ghost_low = split2(recv_a[...].T)
    gather_parts[:, 0 : 4 * GH] = ghost_high
    gather_parts[:, 4 * GH : 8 * GH] = ghost_low

    sums2 = parts
    sums2[...] = jnp.zeros_like(sums2)

    def second_forward(chunk, _):
        far_hot = hot[chunk, A:EXT, :]
        pairs[chunk] += mm(gather_parts[...], jnp.concatenate([far_hot, far_hot], axis=0))
        total = [jnp.zeros((C, A), F32) for _ in range(4)]
        for j in range(CH):
            cut = slice(j * A, (j + 1) * A)
            at = pl.ds(pl.multiple_of(chunk * W + j * A, A), A)
            w = geo[3:4, at]
            u = [geo[a : a + 1, at] for a in range(3)]
            wx = pairs[chunk, 0:C, cut] * w
            wy = [pairs[chunk, (a + 1) * C : (a + 2) * C, cut] * w for a in range(3)]
            along = wy[0] * u[0] + wy[1] * u[1] + wy[2] * u[2]
            total[0] += radial2[chunk, 0:C, cut] * wx + radial2[chunk, 3 * C : 4 * C, cut] * along
            r1x = radial2[chunk, C : 2 * C, cut] * wx
            r2 = radial2[chunk, 2 * C : 3 * C, cut]
            for a in range(3):
                total[a + 1] += r1x * u[a] + r2 * wy[a]
        for a in range(4):
            sums2[a] += total[a]
        return 0

    lax.fori_loop(0, NCH, second_forward, 0)

    b0 = sums2[0]
    b1 = [sums2[1], sums2[2], sums2[3]]
    square2 = b1[0] * b1[0] + b1[1] * b1[1] + b1[2] * b1[2]
    s2 = s1 + mix(node_two[2], b0) + mix(node_two[3], b0 * b0) + mix(node_two[4], square2)
    inner = jnp.concatenate([readout_hidden[...], jnp.zeros((C - 16, C), F32)], axis=0)
    pre = mix(inner, s2)
    gate2 = logistic(pre)
    hidden = pre * gate2
    shift = jnp.zeros((1, A), F32)
    mass = jnp.zeros((1, A), F32)
    for s in range(8):
        shift = jnp.where(species[...] == s, energy_shift[s], shift)
        mass = jnp.where(species[...] == s, masses[s], mass)
    packed_out[0:1, :] = (
        shift + jnp.sum(linear * s1, axis=0, keepdims=True) + jnp.sum(outer * hidden, axis=0, keepdims=True)
    )
    back_pre = outer * (gate2 + hidden * (1.0 - gate2))
    back_s2 = mix(inner.T, back_pre)
    back_b0 = mix(node_two[2].T, back_s2) + 2.0 * b0 * mix(node_two[3].T, back_s2)
    back_square2 = 2.0 * mix(node_two[4].T, back_s2)
    sums2[0] = back_b0
    for a in range(3):
        sums2[a + 1] = b1[a] * back_square2


    def second_back(side, chunk):
        for j in range(CH):
            cut = slice(j * A, (j + 1) * A)
            far = slice(W + j * A, W + (j + 1) * A)
            at = pl.ds(chunk * W + j * A, A)
            w = geo[3:4, at]
            wu = [w * geo[a : a + 1, at] for a in range(3)]
            r3 = radial2[chunk, 3 * C : 4 * C, cut]
            r2 = radial2[chunk, 2 * C : 3 * C, cut]

            def vector_part(a):
                return r3 * (sums2[0] * wu[a]) + r2 * (sums2[a + 1] * w)

            if side == 0:
                dot_u = sums2[1] * wu[0] + sums2[2] * wu[1] + sums2[3] * wu[2]
                back = [
                    radial2[chunk, 0:C, cut] * (sums2[0] * w) + radial2[chunk, C : 2 * C, cut] * dot_u,
                    vector_part(0),
                ]
            else:
                back = [vector_part(1), vector_part(2)]
            for a in range(2):
                h, l = split2(back[a])
                kept = slice(a * C, (a + 1) * C)
                packed[side, chunk, kept, cut] = h
                packed[side, chunk, kept, far] = l
        return mm_nt(hot[chunk], packed[side, chunk, :, 0:W]) + mm_nt(hot[chunk], packed[side, chunk, :, W : 2 * W])

    copies_b = []
    for side in range(2):
        half = pl.ds(side * 2 * C, 2 * C)
        gathered = second_back(side, 0)
        for chunk in range(1, NCH):
            gathered += second_back(side, chunk)
        scat[:, half] = gathered
        copies_b += exchange(
            1 + side, lambda q: scat.at[pl.ds(A + q * GH, GH), half], lambda q: recv_b.at[rows(q), half]
        )

    def second_edges(chunk, _):
        for j in range(CH):
            cut = slice(j * A, (j + 1) * A)
            far = slice(W + j * A, W + (j + 1) * A)
            at = pl.ds(pl.multiple_of(chunk * W + j * A, A), A)
            w = geo[3:4, at]
            u = [geo[a : a + 1, at] for a in range(3)]
            k0 = sums2[0]
            k1 = [sums2[a + 1] for a in range(3)]
            x = pairs[chunk, 0:C, cut]
            y = [pairs[chunk, (a + 1) * C : (a + 2) * C, cut] for a in range(3)]
            dot_u = k1[0] * u[0] + k1[1] * u[1] + k1[2] * u[2]
            along = y[0] * u[0] + y[1] * u[1] + y[2] * u[2]
            cross = y[0] * k1[0] + y[1] * k1[1] + y[2] * k1[2]
            stretch = (
                (radial2[chunk, 0:C, far] * k0 + radial2[chunk, C : 2 * C, far] * dot_u) * x
                + radial2[chunk, 3 * C : 4 * C, far] * along * k0
                + radial2[chunk, 2 * C : 3 * C, far] * cross
            )
            gflat[3:4, at] = w * jnp.sum(stretch, axis=0, keepdims=True)
            r3k0 = radial2[chunk, 3 * C : 4 * C, cut] * k0
            r1x = radial2[chunk, C : 2 * C, cut] * x
            for a in range(3):
                gflat[a : a + 1, at] = w * jnp.sum(r3k0 * y[a] + r1x * k1[a], axis=0, keepdims=True)
        return 0

    lax.fori_loop(0, NCH, second_edges, 0)

    for copy in copies_b:
        copy.wait_recv()
    back_high, back_low = split2(recv_b[...])
    back_table = (scat[0:A] + mm(sent_columns, back_high) + mm(sent_columns, back_low)).T
    back_s1 = back_s2 + linear + mix(node_two[0].T, back_table[0:C])
    back_v1 = mix(
        node_two[1].T, jnp.concatenate([back_table[(a + 1) * C : (a + 2) * C] for a in range(3)], axis=1)
    )
    back_turned = mix(node_one[4].T, back_v1)
    back_square = 2.0 * mix(node_one[3].T, back_s1)
    cut_v = [back_v1[:, a * A : (a + 1) * A] for a in range(3)]
    back_gate = a1[0] * cut_v[0] + a1[1] * cut_v[1] + a1[2] * cut_v[2]
    sums[0] = (
        mix(node_one[1].T, back_s1) + 2.0 * a0 * mix(node_one[2].T, back_s1) + mix(node_one[5].T, back_gate)
    )
    for a in range(3):
        sums[a + 1] = back_turned[:, a * A : (a + 1) * A] + gate1 * cut_v[a] + a1[a] * back_square

    push[...] = jnp.zeros_like(push)

    def first_edges(chunk, _):
        pieces = []
        for j in range(CH):
            cut = slice(j * A, (j + 1) * A)
            at = pl.ds(pl.multiple_of(chunk * W + j * A, A), A)
            u = [geo[a : a + 1, at] for a in range(3)]
            inverse_d = geo[5:6, at]
            k1 = [sums[a + 1] for a in range(3)]
            q1 = kept1[chunk, 0:C, cut]
            dot_u = k1[0] * u[0] + k1[1] * u[1] + k1[2] * u[2]
            stretch = gflat[3:4, at] + jnp.sum(
                kept1[chunk, C : 2 * C, cut] * sums[0] + kept1[chunk, 2 * C : 3 * C, cut] * dot_u,
                axis=0,
                keepdims=True,
            )
            turn = [gflat[a : a + 1, at] + jnp.sum(q1 * k1[a], axis=0, keepdims=True) for a in range(3)]
            inward = turn[0] * u[0] + turn[1] * u[1] + turn[2] * u[2]
            radial_part = stretch - inward * inverse_d
            for a in range(3):
                gflat[a : a + 1, at] = radial_part * u[a] + turn[a] * inverse_d
            gflat[3:8, at] = jnp.zeros((5, A), F32)
        g = gflat[:, lanes_of(chunk)]
        g_high = g.astype(BF16).astype(F32)
        both = jnp.concatenate([g_high, g - g_high], axis=0).astype(BF16)
        push[...] += mm_nt(hot[chunk], both)
        return 0

    lax.fori_loop(0, NCH, first_edges, 0, unroll=True)
    pushed = push[...]
    pushed = pushed[:, 0:8] + pushed[:, 8:16]
    push[:, 0:8] = pushed
    copies_c = exchange(3, lambda q: push.at[pl.ds(A + q * GH, GH)], lambda q: recv_c.at[rows(q)])

    own = jnp.zeros((8, A), F32)
    virial = [[jnp.zeros((1, A), F32) for _ in range(3)] for _ in range(3)]
    for k in range(K):
        own += gflat[:, k * A : (k + 1) * A]
        for a in range(3):
            for b in range(3):
                virial[a][b] += edges[a, k : k + 1, :] * gflat[b : b + 1, k * A : (k + 1) * A]
    for copy in copies_c:
        copy.wait_recv()
    come_high, come_low = split2(recv_c[...])
    back_f = (push[0:A] + mm(sent_columns, come_high) + mm(sent_columns, come_low)).T
    forces = own[0:3] - back_f[0:3]
    packed_out[8:11, :] = forces
    new_velocities = velocities[...] + time_step * forces / mass
    packed_out[16:19, :] = new_velocities

    order = (1, 0, 3, 2)
    movers = jnp.full((1, A), -1, jnp.int32)
    for q in range(4):
        for j in range(4):
            movers = jnp.where(lane == 4 * q + j, migrants[order[q], j], movers)
    chosen = (lax.broadcasted_iota(jnp.int32, (A, A), 0) == movers).astype(F32).astype(BF16)
    state = jnp.concatenate([positions[...], new_velocities, jnp.zeros((2, A), F32)], axis=0)
    h, m, l = split3(state)
    sent_state = mm(jnp.concatenate([h, m, l, jnp.zeros_like(h)], axis=0).astype(BF16), chosen)
    send_d[...] = sent_state[0:8] + sent_state[8:16] + sent_state[16:24]
    copies_d = exchange(4, lambda q: send_d, lambda q: recv_d.at[q])

    mine = jnp.zeros((1, A), F32)
    for a in range(3):
        for b in range(3):
            term = new_velocities[a : a + 1] * mass * new_velocities[b : b + 1] - virial[a][b]
            mine = jnp.where(lane == 3 * a + b, jnp.sum(term, axis=1, keepdims=True), mine)

    def all_sum(number, value, part, stage, many, me, peer):
        part[...] = value.reshape(1, 1, A)
        stage[pl.ds(me, 1)] = value.reshape(1, 1, A)

        @pl.loop(1, many)
        def _(step):
            pltpu.make_async_remote_copy(
                src_ref=part,
                dst_ref=stage.at[pl.ds(me, 1)],
                send_sem=sum_send.at[number],
                recv_sem=sum_recv.at[number],
                device_id=peer(step),
                device_id_type=MESH,
            ).start()

        whole = stage.at[pl.ds(0, many - 1)]
        pltpu.make_async_copy(whole, whole, sum_recv.at[number]).wait()
        pltpu.make_async_copy(whole, whole, sum_send.at[number]).wait()
        return jnp.sum(stage[...], axis=0)

    near = all_sum(0, mine, part1, stage1, many1, mine1, first_peer)
    stress_row = all_sum(1, near, part2, stage2, many2, high, second_peer)

    def entry(ref, a, b):
        return jnp.full((1, A), ref[a, b], F32)

    def determinant(m):
        return (
            m[0][0] * (m[1][1] * m[2][2] - m[1][2] * m[2][1])
            - m[0][1] * (m[1][0] * m[2][2] - m[1][2] * m[2][0])
            + m[0][2] * (m[1][0] * m[2][1] - m[1][1] * m[2][0])
        )

    def inverse(m):
        det = determinant(m)
        cof = [
            [
                m[(r + 1) % 3][(c + 1) % 3] * m[(r + 2) % 3][(c + 2) % 3]
                - m[(r + 1) % 3][(c + 2) % 3] * m[(r + 2) % 3][(c + 1) % 3]
                for c in range(3)
            ]
            for r in range(3)
        ]
        return [[cof[c][r] / det for c in range(3)] for r in range(3)]

    box = [[entry(box_matrix, a, b) for b in range(3)] for a in range(3)]
    volume = determinant(box)
    inv = inverse(box)
    total_atoms = box_mass * (A * slabs * subs)
    pressed = []
    for a in range(3):
        line = []
        for b in range(3):
            value = jnp.broadcast_to(stress_row[:, 3 * a + b : 3 * a + b + 1], (1, A))
            line.append(value - outside_pressure * volume if a == b else value)
        pressed.append(line)
    box_speed = []
    for a in range(3):
        line = []
        for b in range(3):
            pushed_box = pressed[a][0] * inv[b][0] + pressed[a][1] * inv[b][1] + pressed[a][2] * inv[b][2]
            line.append(entry(box_velocity, a, b) + time_step * pushed_box / total_atoms)
        box_speed.append(line)
    new_box = [[box[a][b] + time_step * box_speed[a][b] for b in range(3)] for a in range(3)]
    new_inverse = inverse(new_box)
    for group_at, matrix in ((40, new_box), (48, box_speed)):
        for a in range(3):
            line = jnp.where(lane == 0, matrix[a][0], jnp.where(lane == 1, matrix[a][1], matrix[a][2]))
            packed_out[group_at + a : group_at + a + 1, :] = line

    def drift(moving):
        return [
            new_inverse[a][0] * moving[0:1] + new_inverse[a][1] * moving[1:2] + new_inverse[a][2] * moving[2:3]
            for a in range(3)
        ]

    moved = drift(new_velocities)
    for a in range(3):
        packed_out[24 + a : 25 + a, :] = positions[a : a + 1, :] + time_step * moved[a]
    for copy in copies_d:
        copy.wait_recv()
    come = jnp.where(
        lane < 4, recv_d[0], jnp.where(lane < 8, recv_d[1], jnp.where(lane < 12, recv_d[2], recv_d[3]))
    )
    moved = drift(come[3:6])
    for a in range(3):
        packed_out[32 + a : 33 + a, :] = come[a : a + 1] + time_step * moved[a]
    packed_out[35:38, :] = come[3:6]

    for copies in (copies_a, copies_b, copies_c, copies_d):
        for copy in copies:
            copy.wait_send()


def unpack(held, *outs):
    for i, out in enumerate(outs):
        out[...] = held[8 * i : 8 * i + out.shape[0], 0 : out.shape[1]]


def solution(mesh):
    slabs, subs = mesh.shape["slab"], mesh.shape["sub"]
    many1, many2 = LO * subs, slabs // LO
    vmem = pl.BlockSpec(memory_space=pltpu.VMEM)
    smem = pl.BlockSpec(memory_space=pltpu.SMEM)
    in_smem = {9, 11, 12, 24, 25}

    def body(*arrays):
        arrays = list(arrays)
        for position in (2, 3, 21, 23):
            arrays[position] = arrays[position].reshape(1, -1)
        for position in (13, 15, 17, 19):
            arrays[position] = arrays[position].T
        shapes = [(1, A), (3, A), (3, A), (3, A), (6, 16), (3, 3), (3, 3)]
        held = pl.pallas_call(
            functools.partial(kernel, slabs, subs),
            out_shape=jax.ShapeDtypeStruct((8 * len(shapes), A), F32),
            in_specs=[smem if i in in_smem else vmem for i in range(26)],
            out_specs=vmem,
            scratch_shapes=[
                pltpu.VMEM((8, 128), F32),
                pltpu.VMEM((8, E), F32),
                pltpu.VMEM((K, A), jnp.int32),
                pltpu.VMEM((NCH, 48, 2 * W), BF16),
                pltpu.VMEM((NCH, EXT, W), BF16),
                pltpu.VMEM((NCH, 3 * C, W), F32),
                pltpu.VMEM((NCH, 3 * RH, W), F32),
                pltpu.VMEM((2 * C, W), F32),
                pltpu.VMEM((NCH, 4 * C, 2 * W), F32),
                pltpu.VMEM((4, C, A), F32),
                pltpu.VMEM((NCH, 4 * C, W), F32),
                pltpu.VMEM((4 * C, 2 * A), BF16),
                pltpu.VMEM((4, C, A), F32),
                pltpu.VMEM((4 * C, 8 * GH), BF16),
                pltpu.VMEM((2, NCH, 2 * C, 2 * W), BF16),
                pltpu.VMEM((8, E), F32),
                pltpu.VMEM((4 * GH, 4 * C), F32),
                pltpu.VMEM((4 * GH, 4 * C), F32),
                pltpu.VMEM((EXT, 4 * C), F32),
                pltpu.VMEM((4 * GH, 4 * C), F32),
                pltpu.VMEM((EXT, 16), F32),
                pltpu.VMEM((4 * GH, 16), F32),
                pltpu.VMEM((8, A), F32),
                pltpu.VMEM((4, 8, A), F32),
                pltpu.VMEM((many1, 1, A), F32),
                pltpu.VMEM((many2, 1, A), F32),
                pltpu.VMEM((1, 1, A), F32),
                pltpu.VMEM((1, 1, A), F32),
                pltpu.SemaphoreType.DMA((5, 4)),
                pltpu.SemaphoreType.DMA((5, 4)),
                pltpu.SemaphoreType.DMA((2,)),
                pltpu.SemaphoreType.DMA((2,)),
            ],
            compiler_params=pltpu.CompilerParams(
                collective_id=0, has_side_effects=True, vmem_limit_bytes=56 * 1024 * 1024
            ),
            name="step",
        )(*arrays)
        outs = pl.pallas_call(
            unpack,
            out_shape=[jax.ShapeDtypeStruct(shape, F32) for shape in shapes],
            in_specs=[vmem],
            out_specs=[vmem] * 7,
            name="unpack",
        )(held)
        return (outs[0].reshape(A),) + tuple(outs[1:])

    tail = P(None, ("slab", "sub"))
    flat = P(("slab", "sub"))
    placed = (tail, tail, flat, flat, tail, tail, P(None, None, ("slab", "sub")), tail, tail, tail) + (P(),) * 16
    return jax.shard_map(
        body,
        mesh=mesh,
        in_specs=placed,
        out_specs=(flat, tail, tail, tail, tail, P(), P()),
        check_vma=False,
    )
```

```python
import functools
import math

import jax
import jax.numpy as jnp
from jax import lax
from jax.experimental import pallas as pl
from jax.experimental.pallas import tpu as pltpu
from jax.sharding import PartitionSpec as P

MESH = pl.DeviceIdType.MESH
F32 = jnp.float32
BF16 = jnp.bfloat16
HIGHEST = lax.Precision.HIGHEST

cutoff = 5.0
neighbor_norm = 0.125
time_step = 0.5
outside_pressure = 0.5
box_mass = 0.125

C = 128
A = 128
K = 20
GH = 48
EXT = A + 4 * GH
CH = 4
NCH = K // CH
W = CH * A
E = K * A
RH = 64
LO = 2


def split2(x):
    high = x.astype(BF16)
    return high, (x - high.astype(F32)).astype(BF16)


def split3(x):
    high = x.astype(BF16).astype(F32)
    rest = x - high
    middle = rest.astype(BF16).astype(F32)
    return high, middle, rest - middle


def stack_left(weights):
    high, low = split2(weights)
    return jnp.concatenate([high, high, low], axis=1)


def stack_right(values):
    high, low = split2(values)
    return jnp.concatenate([high, low, high], axis=0)


def stack_basis(weights):
    h, m, l = split3(weights)
    return jnp.concatenate([h, h, h, m, m, l], axis=0).T.astype(BF16)


def stack_out(weights):
    high = weights.astype(BF16).astype(F32)
    return jnp.concatenate([high, high, weights - high], axis=0).T.astype(BF16)


def sine_cosine(turns):
    whole = jnp.floor(turns + 0.5)
    sign = 1.0 - 2.0 * (whole - 2.0 * jnp.floor(0.5 * whole))
    angle = (turns - whole) * math.pi
    square = angle * angle
    sine, cosine = jnp.zeros_like(square), jnp.zeros_like(square)
    for power in range(6, -1, -1):
        flip = (-1) ** power
        sine = sine * square + flip / math.factorial(2 * power + 1)
        cosine = cosine * square + flip / math.factorial(2 * power)
    return sine * angle * sign, cosine * sign


def mm(left, right):
    return jnp.dot(left, right, preferred_element_type=F32)


def mm_nt(left, right):
    return lax.dot_general(left, right, (((1,), (1,)), ((), ())), preferred_element_type=F32)


def mix(weights, values):
    return mm(stack_left(weights), stack_right(values))


def logistic(x):
    return 0.5 + 0.5 * jnp.tanh(0.5 * x)


def radial_net(start, win, mid0, mid1, out):
    pre = mm(win, start)
    for after in (mid0, mid1, out):
        half = pre.shape[1] // 2
        value, slope = pre[:, :half], pre[:, half:]
        gate = logistic(value)
        active = value * gate
        moved = (gate + active * (1.0 - gate)) * slope
        pre = mm(after, stack_right(jnp.concatenate([active, moved], axis=1)))
    return pre


def kernel(slabs, subs, *refs):
    (
        positions, velocities, species, ghost_species, neighbours, slot_mask, edges, send_slab, send_sub, migrants,
        embedding, energy_shift, masses, one_in, one_mid, one_out, node_one, two_in, two_mid, two_out, node_two,
        readout_linear, readout_hidden, readout_out, box_matrix, box_velocity,
        packed_out,
        lists, geo, element, basis, hot, kept1, slopes1, radial1, radial2, sums, pairs, table, parts, gather_parts,
        packed, gflat, send_a, recv_a, scat, recv_b, push, recv_c, send_d, recv_d, stage1, stage2,
        part1, part2, send_sem, recv_sem, sum_send, sum_recv,
    ) = refs
    slab, sub = lax.axis_index("slab"), lax.axis_index("sub")
    low, high = lax.rem(slab, LO), slab // LO
    many1, many2 = LO * subs, slabs // LO
    mine1 = low * subs + sub

    def first_peer(step):
        flat = lax.rem(mine1 + step, many1)
        return (high * LO + flat // subs, lax.rem(flat, subs))

    def second_peer(step):
        return (lax.rem(high + step, many2) * LO + low, sub)

    around = (
        (lax.rem(slab + slabs - 1, slabs), sub),
        (lax.rem(slab + 1, slabs), sub),
        (slab, lax.rem(sub + subs - 1, subs)),
        (slab, lax.rem(sub + 1, subs)),
    )
    barrier = pltpu.get_barrier_semaphore()

    def greet(device):
        pl.semaphore_signal(barrier, inc=1, device_id=device, device_id_type=MESH)

    for device in around:
        greet(device)

    @pl.loop(1, many1)
    def _(step):
        greet(first_peer(step))

    @pl.loop(1, many2)
    def _(step):
        greet(second_peer(step))

    def exchange(number, source, target):
        copies = []
        for block in (2, 3, 0, 1):
            copy = pltpu.make_async_remote_copy(
                src_ref=source(block),
                dst_ref=target(block ^ 1),
                send_sem=send_sem.at[number, block],
                recv_sem=recv_sem.at[number, block ^ 1],
                device_id=around[block],
                device_id_type=MESH,
            )
            copy.start()
            copies.append(copy)
        return copies

    def rows(block):
        return pl.ds(block * GH, GH)

    lane = lax.broadcasted_iota(jnp.int32, (1, A), 1)

    lists[...] = jnp.zeros_like(lists)
    lists[0:2, 0:GH] = send_slab[...].astype(F32)
    lists[2:4, 0:GH] = send_sub[...].astype(F32)
    lists[4:5, 0:16] = readout_out[...]
    lists[5:6, :] = readout_linear[...]
    columns = lists[...].T
    outer = jnp.broadcast_to(columns[:, 4:5], (C, A))
    linear = jnp.broadcast_to(columns[:, 5:6], (C, A))
    lanes_f = lax.broadcasted_iota(jnp.int32, (GH, A), 1).astype(F32)
    sent_f = jnp.concatenate(
        [(lanes_f == columns[0:GH, q : q + 1]).astype(F32) for q in range(4)], axis=0
    )
    sent_rows = sent_f.astype(BF16)
    sent_columns = sent_f.T.astype(BF16)

    ex, ey, ez = edges[0], edges[1], edges[2]
    distance = jnp.sqrt(ex * ex + ey * ey + ez * ez)
    inverse_distance = 1.0 / distance
    unit = (ex / distance, ey / distance, ez / distance)
    weight = slot_mask[...].astype(F32) * neighbor_norm
    for row, values in enumerate(unit + (weight, distance, inverse_distance)):
        for k in range(K):
            geo[row : row + 1, k * A : (k + 1) * A] = values[k : k + 1, :]

    kinds = lax.broadcasted_iota(jnp.int32, (8, A), 0)
    own_kind = (kinds == species[...]).astype(F32)
    pad8 = jnp.zeros((8, A), F32)
    near = neighbours[...]
    spot, group = near & (A - 1), near >> 7

    def look_up(row):
        spread = jnp.broadcast_to(row, (K, A))
        return jnp.take_along_axis(spread, spot, axis=1, mode="promise_in_bounds")

    ghosts = ghost_species[...]
    tail = jnp.concatenate([ghosts[:, A:], jnp.zeros((1, 2 * A - 4 * GH), jnp.int32)], axis=1)
    element[...] = jnp.where(
        group == 0, look_up(species[...]), jnp.where(group == 1, look_up(ghosts[:, 0:A]), look_up(tail))
    )

    orders = (lax.broadcasted_iota(jnp.int32, (8, 1), 0) + 1).astype(F32)
    scale = jnp.sqrt(2.0 / cutoff).astype(F32)

    one_in_s = stack_basis(one_in[...])
    one_mid0, one_mid1 = stack_left(one_mid[0]), stack_left(one_mid[1])
    one_out_s = stack_out(one_out[...])

    lifted = lax.dot_general(
        embedding[...], node_one[0], (((1,), (1,)), ((), ())), precision=HIGHEST, preferred_element_type=F32
    )
    lifted_s = jnp.concatenate(list(split3(lifted)) + [pad8], axis=0).T.astype(BF16)

    sums[...] = jnp.zeros_like(sums)

    def lanes_of(chunk):
        return pl.ds(pl.multiple_of(chunk * W, W), W)

    def first_forward(chunk, _):
        here = lanes_of(chunk)
        d = geo[4:5, here]
        inverse_d = geo[5:6, here]
        x = d / cutoff
        x2 = x * x
        x3 = x2 * x
        x5 = x2 * x3
        x6 = x3 * x3
        envelope = 1.0 - 28.0 * x6 + 48.0 * x6 * x - 21.0 * x6 * x2
        slope = (-168.0 * x5 + 336.0 * x6 - 168.0 * x6 * x) / cutoff
        sine, cosine = sine_cosine(orders * x)
        even = scale * inverse_d * envelope
        values = sine * even
        slopes = cosine * (orders * (math.pi / cutoff)) * even + sine * (
            scale * inverse_d * (slope - envelope * inverse_d)
        )
        h, m, l = split3(jnp.concatenate([values, slopes], axis=1))
        start = jnp.concatenate([h, m, l, h, m, h], axis=0).astype(BF16)
        basis[chunk] = start
        pre = mm(one_in_s, start[:, 0:W])
        for layer, after in enumerate((one_mid0, one_mid1, one_out_s)):
            gate = logistic(pre)
            active = pre * gate
            slopes1[chunk, layer * RH : (layer + 1) * RH] = gate + active * (1.0 - gate)
            pre = mm(after, stack_right(active))
        radial1[...] = pre
        kind8 = jnp.concatenate(
            [(kinds == element[pl.ds(chunk * CH + j, 1), :]).astype(F32) for j in range(CH)], axis=1
        )
        picked_x = mm(lifted_s, jnp.concatenate([kind8, kind8, kind8, jnp.zeros_like(kind8)], axis=0).astype(BF16))
        total = [jnp.zeros((C, A), F32) for _ in range(4)]
        for j in range(CH):
            cut = slice(j * A, (j + 1) * A)
            at = pl.ds(pl.multiple_of(chunk * W + j * A, A), A)
            wx = picked_x[:, cut] * geo[3:4, at]
            total[0] += radial1[0:C, cut] * wx
            q1 = radial1[C : 2 * C, cut] * wx
            for a in range(3):
                total[a + 1] += geo[a : a + 1, at] * q1
            kept1[chunk, 0:C, cut] = q1
            kept1[chunk, C : 2 * C, cut] = wx
        for a in range(4):
            sums[a] += total[a]
        return 0

    def first_slopes(chunk, _):
        pre = mm(one_in_s, basis[chunk, :, W : 2 * W])
        for layer, after in enumerate((one_mid0, one_mid1, one_out_s)):
            pre = mm(after, stack_right(slopes1[chunk, layer * RH : (layer + 1) * RH] * pre))
        wx = kept1[chunk, C : 2 * C]
        kept1[chunk, C : 2 * C] = pre[0:C] * wx
        kept1[chunk, 2 * C : 3 * C] = pre[C : 2 * C] * wx
        return 0

    lax.fori_loop(0, NCH, first_forward, 0, unroll=True)

    s0 = mm(
        jnp.concatenate(list(split3(embedding[...])) + [pad8], axis=0).T.astype(BF16),
        jnp.concatenate([own_kind, own_kind, own_kind, pad8], axis=0).astype(BF16),
    )
    a0 = sums[0]
    a1 = [sums[1], sums[2], sums[3]]
    square = a1[0] * a1[0] + a1[1] * a1[1] + a1[2] * a1[2]
    s1 = s0 + mix(node_one[1], a0) + mix(node_one[2], a0 * a0) + mix(node_one[3], square)
    turned = mix(node_one[4], jnp.concatenate(a1, axis=1))
    gate1 = mix(node_one[5], a0)
    v1 = jnp.concatenate([turned[:, a * A : (a + 1) * A] + gate1 * a1[a] for a in range(3)], axis=1)
    lifted_x = mix(node_two[0], s1)
    lifted_y = mix(node_two[1], v1)
    own_table = jnp.concatenate([lifted_x] + [lifted_y[:, a * A : (a + 1) * A] for a in range(3)], axis=0)
    own_high, own_low = split2(own_table)
    send_a[...] = mm_nt(sent_rows, own_high) + mm_nt(sent_rows, own_low)
    table[:, 0:A] = own_high
    table[:, A : 2 * A] = own_low

    pl.semaphore_wait(barrier, 4 + many1 - 1 + many2 - 1)
    copies_a = exchange(0, lambda q: send_a.at[rows(q)], lambda q: recv_a.at[rows(q)])

    two_in_s = stack_basis(two_in[...])
    two_mid0, two_mid1 = stack_left(two_mid[0]), stack_left(two_mid[1])
    two_out_s = stack_out(two_out[...])

    def second_radial(chunk, _):
        row_of = lax.broadcasted_iota(jnp.int32, (EXT, A), 0)
        for j in range(CH):
            picked = neighbours[pl.ds(chunk * CH + j, 1), :]
            hot[chunk, :, j * A : (j + 1) * A] = (row_of == picked).astype(F32).astype(BF16)
        radial2[chunk] = radial_net(basis[chunk], two_in_s, two_mid0, two_mid1, two_out_s)
        own_hot = hot[chunk, 0:A, :]
        pairs[chunk] = mm(table[...], jnp.concatenate([own_hot, own_hot], axis=0))
        return 0

    lax.fori_loop(0, NCH, second_radial, 0, unroll=True)
    lax.fori_loop(0, NCH, first_slopes, 0, unroll=True)

    for copy in copies_a:
        copy.wait_recv()
    ghost_high, ghost_low = split2(recv_a[...].T)
    gather_parts[:, 0 : 4 * GH] = ghost_high
    gather_parts[:, 4 * GH : 8 * GH] = ghost_low

    sums2 = parts
    sums2[...] = jnp.zeros_like(sums2)

    def second_forward(chunk, _):
        far_hot = hot[chunk, A:EXT, :]
        pairs[chunk] += mm(gather_parts[...], jnp.concatenate([far_hot, far_hot], axis=0))
        total = [jnp.zeros((C, A), F32) for _ in range(4)]
        for j in range(CH):
            cut = slice(j * A, (j + 1) * A)
            at = pl.ds(chunk * W + j * A, A)
            w = geo[3:4, at]
            u = [geo[a : a + 1, at] for a in range(3)]
            wx = pairs[chunk, 0:C, cut] * w
            wy = [pairs[chunk, (a + 1) * C : (a + 2) * C, cut] * w for a in range(3)]
            along = wy[0] * u[0] + wy[1] * u[1] + wy[2] * u[2]
            total[0] += radial2[chunk, 0:C, cut] * wx + radial2[chunk, 3 * C : 4 * C, cut] * along
            r1x = radial2[chunk, C : 2 * C, cut] * wx
            r2 = radial2[chunk, 2 * C : 3 * C, cut]
            for a in range(3):
                total[a + 1] += r1x * u[a] + r2 * wy[a]
        for a in range(4):
            sums2[a] += total[a]
        return 0

    def all_second_forward(_, carry):
        for chunk in range(NCH):
            second_forward(chunk, 0)
        return carry

    lax.fori_loop(0, 1 + slab // slabs, all_second_forward, 0)

    b0 = sums2[0]
    b1 = [sums2[1], sums2[2], sums2[3]]
    square2 = b1[0] * b1[0] + b1[1] * b1[1] + b1[2] * b1[2]
    s2 = s1 + mix(node_two[2], b0) + mix(node_two[3], b0 * b0) + mix(node_two[4], square2)
    inner = jnp.concatenate([readout_hidden[...], jnp.zeros((C - 16, C), F32)], axis=0)
    pre = mix(inner, s2)
    gate2 = logistic(pre)
    hidden = pre * gate2
    shift = jnp.zeros((1, A), F32)
    mass = jnp.zeros((1, A), F32)
    for s in range(8):
        shift = jnp.where(species[...] == s, energy_shift[s], shift)
        mass = jnp.where(species[...] == s, masses[s], mass)
    packed_out[0:1, :] = (
        shift + jnp.sum(linear * s1, axis=0, keepdims=True) + jnp.sum(outer * hidden, axis=0, keepdims=True)
    )
    back_pre = outer * (gate2 + hidden * (1.0 - gate2))
    back_s2 = mix(inner.T, back_pre)
    back_b0 = mix(node_two[2].T, back_s2) + 2.0 * b0 * mix(node_two[3].T, back_s2)
    back_square2 = 2.0 * mix(node_two[4].T, back_s2)
    sums2[0] = back_b0
    for a in range(3):
        sums2[a + 1] = b1[a] * back_square2


    def second_back(side, chunk):
        for j in range(CH):
            cut = slice(j * A, (j + 1) * A)
            far = slice(W + j * A, W + (j + 1) * A)
            at = pl.ds(chunk * W + j * A, A)
            w = geo[3:4, at]
            wu = [w * geo[a : a + 1, at] for a in range(3)]
            r3 = radial2[chunk, 3 * C : 4 * C, cut]
            r2 = radial2[chunk, 2 * C : 3 * C, cut]

            def vector_part(a):
                return r3 * (sums2[0] * wu[a]) + r2 * (sums2[a + 1] * w)

            if side == 0:
                dot_u = sums2[1] * wu[0] + sums2[2] * wu[1] + sums2[3] * wu[2]
                back = [
                    radial2[chunk, 0:C, cut] * (sums2[0] * w) + radial2[chunk, C : 2 * C, cut] * dot_u,
                    vector_part(0),
                ]
            else:
                back = [vector_part(1), vector_part(2)]
            for a in range(2):
                h, l = split2(back[a])
                kept = slice(a * C, (a + 1) * C)
                packed[side, chunk, kept, cut] = h
                packed[side, chunk, kept, far] = l
        return mm_nt(hot[chunk], packed[side, chunk, :, 0:W]) + mm_nt(hot[chunk], packed[side, chunk, :, W : 2 * W])

    copies_b = []
    for side in range(2):
        half = pl.ds(side * 2 * C, 2 * C)
        gathered = second_back(side, 0)
        for chunk in range(1, NCH):
            gathered += second_back(side, chunk)
        scat[:, half] = gathered
        copies_b += exchange(
            1 + side, lambda q: scat.at[pl.ds(A + q * GH, GH), half], lambda q: recv_b.at[rows(q), half]
        )

    def second_edges(chunk, _):
        for j in range(CH):
            cut = slice(j * A, (j + 1) * A)
            far = slice(W + j * A, W + (j + 1) * A)
            at = pl.ds(pl.multiple_of(chunk * W + j * A, A), A)
            w = geo[3:4, at]
            u = [geo[a : a + 1, at] for a in range(3)]
            k0 = sums2[0]
            k1 = [sums2[a + 1] for a in range(3)]
            x = pairs[chunk, 0:C, cut]
            y = [pairs[chunk, (a + 1) * C : (a + 2) * C, cut] for a in range(3)]
            dot_u = k1[0] * u[0] + k1[1] * u[1] + k1[2] * u[2]
            along = y[0] * u[0] + y[1] * u[1] + y[2] * u[2]
            cross = y[0] * k1[0] + y[1] * k1[1] + y[2] * k1[2]
            stretch = (
                (radial2[chunk, 0:C, far] * k0 + radial2[chunk, C : 2 * C, far] * dot_u) * x
                + radial2[chunk, 3 * C : 4 * C, far] * along * k0
                + radial2[chunk, 2 * C : 3 * C, far] * cross
            )
            gflat[3:4, at] = w * jnp.sum(stretch, axis=0, keepdims=True)
            r3k0 = radial2[chunk, 3 * C : 4 * C, cut] * k0
            r1x = radial2[chunk, C : 2 * C, cut] * x
            for a in range(3):
                gflat[a : a + 1, at] = w * jnp.sum(r3k0 * y[a] + r1x * k1[a], axis=0, keepdims=True)
        return 0

    lax.fori_loop(0, NCH, second_edges, 0)

    for copy in copies_b:
        copy.wait_recv()
    back_high, back_low = split2(recv_b[...])
    back_table = (scat[0:A] + mm(sent_columns, back_high) + mm(sent_columns, back_low)).T
    back_s1 = back_s2 + linear + mix(node_two[0].T, back_table[0:C])
    back_v1 = mix(
        node_two[1].T, jnp.concatenate([back_table[(a + 1) * C : (a + 2) * C] for a in range(3)], axis=1)
    )
    back_turned = mix(node_one[4].T, back_v1)
    back_square = 2.0 * mix(node_one[3].T, back_s1)
    cut_v = [back_v1[:, a * A : (a + 1) * A] for a in range(3)]
    back_gate = a1[0] * cut_v[0] + a1[1] * cut_v[1] + a1[2] * cut_v[2]
    sums[0] = (
        mix(node_one[1].T, back_s1) + 2.0 * a0 * mix(node_one[2].T, back_s1) + mix(node_one[5].T, back_gate)
    )
    for a in range(3):
        sums[a + 1] = back_turned[:, a * A : (a + 1) * A] + gate1 * cut_v[a] + a1[a] * back_square

    push[...] = jnp.zeros_like(push)

    def first_edges(chunk, _):
        pieces = []
        for j in range(CH):
            cut = slice(j * A, (j + 1) * A)
            at = pl.ds(pl.multiple_of(chunk * W + j * A, A), A)
            u = [geo[a : a + 1, at] for a in range(3)]
            inverse_d = geo[5:6, at]
            k1 = [sums[a + 1] for a in range(3)]
            q1 = kept1[chunk, 0:C, cut]
            dot_u = k1[0] * u[0] + k1[1] * u[1] + k1[2] * u[2]
            stretch = gflat[3:4, at] + jnp.sum(
                kept1[chunk, C : 2 * C, cut] * sums[0] + kept1[chunk, 2 * C : 3 * C, cut] * dot_u,
                axis=0,
                keepdims=True,
            )
            turn = [gflat[a : a + 1, at] + jnp.sum(q1 * k1[a], axis=0, keepdims=True) for a in range(3)]
            inward = turn[0] * u[0] + turn[1] * u[1] + turn[2] * u[2]
            radial_part = stretch - inward * inverse_d
            for a in range(3):
                gflat[a : a + 1, at] = radial_part * u[a] + turn[a] * inverse_d
            gflat[3:8, at] = jnp.zeros((5, A), F32)
        g = gflat[:, lanes_of(chunk)]
        g_high = g.astype(BF16).astype(F32)
        both = jnp.concatenate([g_high, g - g_high], axis=0).astype(BF16)
        push[...] += mm_nt(hot[chunk], both)
        return 0

    lax.fori_loop(0, NCH, first_edges, 0, unroll=True)
    pushed = push[...]
    pushed = pushed[:, 0:8] + pushed[:, 8:16]
    push[:, 0:8] = pushed
    copies_c = exchange(3, lambda q: push.at[pl.ds(A + q * GH, GH)], lambda q: recv_c.at[rows(q)])

    own = jnp.zeros((8, A), F32)
    virial = [[jnp.zeros((1, A), F32) for _ in range(3)] for _ in range(3)]
    for k in range(K):
        own += gflat[:, k * A : (k + 1) * A]
        for a in range(3):
            for b in range(3):
                virial[a][b] += edges[a, k : k + 1, :] * gflat[b : b + 1, k * A : (k + 1) * A]
    for copy in copies_c:
        copy.wait_recv()
    come_high, come_low = split2(recv_c[...])
    back_f = (push[0:A] + mm(sent_columns, come_high) + mm(sent_columns, come_low)).T
    forces = own[0:3] - back_f[0:3]
    packed_out[8:11, :] = forces
    new_velocities = velocities[...] + time_step * forces / mass
    packed_out[16:19, :] = new_velocities

    order = (1, 0, 3, 2)
    movers = jnp.full((1, A), -1, jnp.int32)
    for q in range(4):
        for j in range(4):
            movers = jnp.where(lane == 4 * q + j, migrants[order[q], j], movers)
    chosen = (lax.broadcasted_iota(jnp.int32, (A, A), 0) == movers).astype(F32).astype(BF16)
    state = jnp.concatenate([positions[...], new_velocities, jnp.zeros((2, A), F32)], axis=0)
    h, m, l = split3(state)
    sent_state = mm(jnp.concatenate([h, m, l, jnp.zeros_like(h)], axis=0).astype(BF16), chosen)
    send_d[...] = sent_state[0:8] + sent_state[8:16] + sent_state[16:24]
    copies_d = exchange(4, lambda q: send_d, lambda q: recv_d.at[q])

    mine = jnp.zeros((1, A), F32)
    for a in range(3):
        for b in range(3):
            term = new_velocities[a : a + 1] * mass * new_velocities[b : b + 1] - virial[a][b]
            mine = jnp.where(lane == 3 * a + b, jnp.sum(term, axis=1, keepdims=True), mine)

    def all_sum(number, value, part, stage, many, me, peer):
        part[...] = value.reshape(1, 1, A)
        stage[pl.ds(me, 1)] = value.reshape(1, 1, A)

        @pl.loop(1, many)
        def _(step):
            pltpu.make_async_remote_copy(
                src_ref=part,
                dst_ref=stage.at[pl.ds(me, 1)],
                send_sem=sum_send.at[number],
                recv_sem=sum_recv.at[number],
                device_id=peer(step),
                device_id_type=MESH,
            ).start()

        whole = stage.at[pl.ds(0, many - 1)]
        pltpu.make_async_copy(whole, whole, sum_recv.at[number]).wait()
        pltpu.make_async_copy(whole, whole, sum_send.at[number]).wait()
        return jnp.sum(stage[...], axis=0)

    near = all_sum(0, mine, part1, stage1, many1, mine1, first_peer)
    stress_row = all_sum(1, near, part2, stage2, many2, high, second_peer)

    def entry(ref, a, b):
        return jnp.full((1, A), ref[a, b], F32)

    def determinant(m):
        return (
            m[0][0] * (m[1][1] * m[2][2] - m[1][2] * m[2][1])
            - m[0][1] * (m[1][0] * m[2][2] - m[1][2] * m[2][0])
            + m[0][2] * (m[1][0] * m[2][1] - m[1][1] * m[2][0])
        )

    def inverse(m):
        det = determinant(m)
        cof = [
            [
                m[(r + 1) % 3][(c + 1) % 3] * m[(r + 2) % 3][(c + 2) % 3]
                - m[(r + 1) % 3][(c + 2) % 3] * m[(r + 2) % 3][(c + 1) % 3]
                for c in range(3)
            ]
            for r in range(3)
        ]
        return [[cof[c][r] / det for c in range(3)] for r in range(3)]

    box = [[entry(box_matrix, a, b) for b in range(3)] for a in range(3)]
    volume = determinant(box)
    inv = inverse(box)
    total_atoms = box_mass * (A * slabs * subs)
    pressed = []
    for a in range(3):
        line = []
        for b in range(3):
            value = jnp.broadcast_to(stress_row[:, 3 * a + b : 3 * a + b + 1], (1, A))
            line.append(value - outside_pressure * volume if a == b else value)
        pressed.append(line)
    box_speed = []
    for a in range(3):
        line = []
        for b in range(3):
            pushed_box = pressed[a][0] * inv[b][0] + pressed[a][1] * inv[b][1] + pressed[a][2] * inv[b][2]
            line.append(entry(box_velocity, a, b) + time_step * pushed_box / total_atoms)
        box_speed.append(line)
    new_box = [[box[a][b] + time_step * box_speed[a][b] for b in range(3)] for a in range(3)]
    new_inverse = inverse(new_box)
    for group_at, matrix in ((40, new_box), (48, box_speed)):
        for a in range(3):
            line = jnp.where(lane == 0, matrix[a][0], jnp.where(lane == 1, matrix[a][1], matrix[a][2]))
            packed_out[group_at + a : group_at + a + 1, :] = line

    def drift(moving):
        return [
            new_inverse[a][0] * moving[0:1] + new_inverse[a][1] * moving[1:2] + new_inverse[a][2] * moving[2:3]
            for a in range(3)
        ]

    moved = drift(new_velocities)
    for a in range(3):
        packed_out[24 + a : 25 + a, :] = positions[a : a + 1, :] + time_step * moved[a]
    for copy in copies_d:
        copy.wait_recv()
    come = jnp.where(
        lane < 4, recv_d[0], jnp.where(lane < 8, recv_d[1], jnp.where(lane < 12, recv_d[2], recv_d[3]))
    )
    moved = drift(come[3:6])
    for a in range(3):
        packed_out[32 + a : 33 + a, :] = come[a : a + 1] + time_step * moved[a]
    packed_out[35:38, :] = come[3:6]

    for copies in (copies_a, copies_b, copies_c, copies_d):
        for copy in copies:
            copy.wait_send()


def unpack(held, *outs):
    for i, out in enumerate(outs):
        out[...] = held[8 * i : 8 * i + out.shape[0], 0 : out.shape[1]]


def solution(mesh):
    slabs, subs = mesh.shape["slab"], mesh.shape["sub"]
    many1, many2 = LO * subs, slabs // LO
    vmem = pl.BlockSpec(memory_space=pltpu.VMEM)
    smem = pl.BlockSpec(memory_space=pltpu.SMEM)
    in_smem = {9, 11, 12, 24, 25}

    def body(*arrays):
        arrays = list(arrays)
        for position in (2, 3, 21, 23):
            arrays[position] = arrays[position].reshape(1, -1)
        for position in (13, 15, 17, 19):
            arrays[position] = arrays[position].T
        shapes = [(1, A), (3, A), (3, A), (3, A), (6, 16), (3, 3), (3, 3)]
        held = pl.pallas_call(
            functools.partial(kernel, slabs, subs),
            out_shape=jax.ShapeDtypeStruct((8 * len(shapes), A), F32),
            in_specs=[smem if i in in_smem else vmem for i in range(26)],
            out_specs=vmem,
            scratch_shapes=[
                pltpu.VMEM((8, 128), F32),
                pltpu.VMEM((8, E), F32),
                pltpu.VMEM((K, A), jnp.int32),
                pltpu.VMEM((NCH, 48, 2 * W), BF16),
                pltpu.VMEM((NCH, EXT, W), BF16),
                pltpu.VMEM((NCH, 3 * C, W), F32),
                pltpu.VMEM((NCH, 3 * RH, W), F32),
                pltpu.VMEM((2 * C, W), F32),
                pltpu.VMEM((NCH, 4 * C, 2 * W), F32),
                pltpu.VMEM((4, C, A), F32),
                pltpu.VMEM((NCH, 4 * C, W), F32),
                pltpu.VMEM((4 * C, 2 * A), BF16),
                pltpu.VMEM((4, C, A), F32),
                pltpu.VMEM((4 * C, 8 * GH), BF16),
                pltpu.VMEM((2, NCH, 2 * C, 2 * W), BF16),
                pltpu.VMEM((8, E), F32),
                pltpu.VMEM((4 * GH, 4 * C), F32),
                pltpu.VMEM((4 * GH, 4 * C), F32),
                pltpu.VMEM((EXT, 4 * C), F32),
                pltpu.VMEM((4 * GH, 4 * C), F32),
                pltpu.VMEM((EXT, 16), F32),
                pltpu.VMEM((4 * GH, 16), F32),
                pltpu.VMEM((8, A), F32),
                pltpu.VMEM((4, 8, A), F32),
                pltpu.VMEM((many1, 1, A), F32),
                pltpu.VMEM((many2, 1, A), F32),
                pltpu.VMEM((1, 1, A), F32),
                pltpu.VMEM((1, 1, A), F32),
                pltpu.SemaphoreType.DMA((5, 4)),
                pltpu.SemaphoreType.DMA((5, 4)),
                pltpu.SemaphoreType.DMA((2,)),
                pltpu.SemaphoreType.DMA((2,)),
            ],
            compiler_params=pltpu.CompilerParams(
                collective_id=0, has_side_effects=True, vmem_limit_bytes=56 * 1024 * 1024
            ),
            name="step",
        )(*arrays)
        outs = pl.pallas_call(
            unpack,
            out_shape=[jax.ShapeDtypeStruct(shape, F32) for shape in shapes],
            in_specs=[vmem],
            out_specs=[vmem] * 7,
            name="unpack",
        )(held)
        return (outs[0].reshape(A),) + tuple(outs[1:])

    tail = P(None, ("slab", "sub"))
    flat = P(("slab", "sub"))
    placed = (tail, tail, flat, flat, tail, tail, P(None, None, ("slab", "sub")), tail, tail, tail) + (P(),) * 16
    return jax.shard_map(
        body,
        mesh=mesh,
        in_specs=placed,
        out_specs=(flat, tail, tail, tail, tail, P(), P()),
        check_vma=False,
    )
```

```python
import functools
import math

import jax
import jax.numpy as jnp
from jax import lax
from jax.experimental import pallas as pl
from jax.experimental.pallas import tpu as pltpu
from jax.sharding import PartitionSpec as P

MESH = pl.DeviceIdType.MESH
F32 = jnp.float32
BF16 = jnp.bfloat16
HIGHEST = lax.Precision.HIGHEST

cutoff = 5.0
neighbor_norm = 0.125
time_step = 0.5
outside_pressure = 0.5
box_mass = 0.125

C = 128
A = 128
K = 20
GH = 48
EXT = A + 4 * GH
CH = 4
NCH = K // CH
W = CH * A
E = K * A
RH = 64
LO = 2


def split2(x):
    high = x.astype(BF16)
    return high, (x - high.astype(F32)).astype(BF16)


def split3(x):
    high = x.astype(BF16).astype(F32)
    rest = x - high
    middle = rest.astype(BF16).astype(F32)
    return high, middle, rest - middle


def stack_left(weights):
    high, low = split2(weights)
    return jnp.concatenate([high, high, low], axis=1)


def stack_right(values):
    high, low = split2(values)
    return jnp.concatenate([high, low, high], axis=0)


def stack_basis(weights):
    h, m, l = split3(weights)
    return jnp.concatenate([h, h, h, m, m, l], axis=0).T.astype(BF16)


def stack_out(weights):
    high = weights.astype(BF16).astype(F32)
    return jnp.concatenate([high, high, weights - high], axis=0).T.astype(BF16)


def sine_cosine(turns):
    whole = jnp.floor(turns + 0.5)
    sign = 1.0 - 2.0 * (whole - 2.0 * jnp.floor(0.5 * whole))
    angle = (turns - whole) * math.pi
    square = angle * angle
    sine, cosine = jnp.zeros_like(square), jnp.zeros_like(square)
    for power in range(6, -1, -1):
        flip = (-1) ** power
        sine = sine * square + flip / math.factorial(2 * power + 1)
        cosine = cosine * square + flip / math.factorial(2 * power)
    return sine * angle * sign, cosine * sign


def mm(left, right):
    return jnp.dot(left, right, preferred_element_type=F32)


def mm_nt(left, right):
    return lax.dot_general(left, right, (((1,), (1,)), ((), ())), preferred_element_type=F32)


def mix(weights, values):
    return mm(stack_left(weights), stack_right(values))


def logistic(x):
    return 0.5 + 0.5 * jnp.tanh(0.5 * x)


def radial_net(start, win, mid0, mid1, out):
    pre = mm(win, start)
    for after in (mid0, mid1, out):
        half = pre.shape[1] // 2
        value, slope = pre[:, :half], pre[:, half:]
        gate = logistic(value)
        active = value * gate
        moved = (gate + active * (1.0 - gate)) * slope
        pre = mm(after, stack_right(jnp.concatenate([active, moved], axis=1)))
    return pre


def kernel(slabs, subs, *refs):
    (
        positions, velocities, species, ghost_species, neighbours, slot_mask, edges, send_slab, send_sub, migrants,
        embedding, energy_shift, masses, one_in, one_mid, one_out, node_one, two_in, two_mid, two_out, node_two,
        readout_linear, readout_hidden, readout_out, box_matrix, box_velocity,
        packed_out,
        lists, geo, element, basis, hot, kept1, slopes1, radial1, radial2, sums, pairs, table, parts, gather_parts,
        packed, gflat, send_a, recv_a, scat, recv_b, push, recv_c, send_d, recv_d, stage1, stage2,
        part1, part2, send_sem, recv_sem, sum_send, sum_recv,
    ) = refs
    slab, sub = lax.axis_index("slab"), lax.axis_index("sub")
    low, high = lax.rem(slab, LO), slab // LO
    many1, many2 = LO * subs, slabs // LO
    mine1 = low * subs + sub

    def first_peer(step):
        flat = lax.rem(mine1 + step, many1)
        return (high * LO + flat // subs, lax.rem(flat, subs))

    def second_peer(step):
        return (lax.rem(high + step, many2) * LO + low, sub)

    around = (
        (lax.rem(slab + slabs - 1, slabs), sub),
        (lax.rem(slab + 1, slabs), sub),
        (slab, lax.rem(sub + subs - 1, subs)),
        (slab, lax.rem(sub + 1, subs)),
    )
    barrier = pltpu.get_barrier_semaphore()

    def greet(device):
        pl.semaphore_signal(barrier, inc=1, device_id=device, device_id_type=MESH)

    for device in around:
        greet(device)

    @pl.loop(1, many1)
    def _(step):
        greet(first_peer(step))

    @pl.loop(1, many2)
    def _(step):
        greet(second_peer(step))

    def exchange(number, source, target):
        copies = []
        for block in (2, 3, 0, 1):
            copy = pltpu.make_async_remote_copy(
                src_ref=source(block),
                dst_ref=target(block ^ 1),
                send_sem=send_sem.at[number, block],
                recv_sem=recv_sem.at[number, block ^ 1],
                device_id=around[block],
                device_id_type=MESH,
            )
            copy.start()
            copies.append(copy)
        return copies

    def rows(block):
        return pl.ds(block * GH, GH)

    lane = lax.broadcasted_iota(jnp.int32, (1, A), 1)

    lists[...] = jnp.zeros_like(lists)
    lists[0:2, 0:GH] = send_slab[...].astype(F32)
    lists[2:4, 0:GH] = send_sub[...].astype(F32)
    lists[4:5, 0:16] = readout_out[...]
    lists[5:6, :] = readout_linear[...]
    columns = lists[...].T
    outer = jnp.broadcast_to(columns[:, 4:5], (C, A))
    linear = jnp.broadcast_to(columns[:, 5:6], (C, A))
    lanes_f = lax.broadcasted_iota(jnp.int32, (GH, A), 1).astype(F32)
    sent_f = jnp.concatenate(
        [(lanes_f == columns[0:GH, q : q + 1]).astype(F32) for q in range(4)], axis=0
    )
    sent_rows = sent_f.astype(BF16)
    sent_columns = sent_f.T.astype(BF16)

    ex, ey, ez = edges[0], edges[1], edges[2]
    distance = jnp.sqrt(ex * ex + ey * ey + ez * ez)
    inverse_distance = 1.0 / distance
    unit = (ex / distance, ey / distance, ez / distance)
    weight = slot_mask[...].astype(F32) * neighbor_norm
    for row, values in enumerate(unit + (weight, distance, inverse_distance)):
        for k in range(K):
            geo[row : row + 1, k * A : (k + 1) * A] = values[k : k + 1, :]

    kinds = lax.broadcasted_iota(jnp.int32, (8, A), 0)
    own_kind = (kinds == species[...]).astype(F32)
    pad8 = jnp.zeros((8, A), F32)
    near = neighbours[...]
    spot, group = near & (A - 1), near >> 7

    def look_up(row):
        spread = jnp.broadcast_to(row, (K, A))
        return jnp.take_along_axis(spread, spot, axis=1, mode="promise_in_bounds")

    ghosts = ghost_species[...]
    tail = jnp.concatenate([ghosts[:, A:], jnp.zeros((1, 2 * A - 4 * GH), jnp.int32)], axis=1)
    element[...] = jnp.where(
        group == 0, look_up(species[...]), jnp.where(group == 1, look_up(ghosts[:, 0:A]), look_up(tail))
    )

    orders = (lax.broadcasted_iota(jnp.int32, (8, 1), 0) + 1).astype(F32)
    scale = jnp.sqrt(2.0 / cutoff).astype(F32)

    one_in_s = stack_basis(one_in[...])
    one_mid0, one_mid1 = stack_left(one_mid[0]), stack_left(one_mid[1])
    one_out_s = stack_out(one_out[...])

    lifted = lax.dot_general(
        embedding[...], node_one[0], (((1,), (1,)), ((), ())), precision=HIGHEST, preferred_element_type=F32
    )
    lifted_s = jnp.concatenate(list(split3(lifted)) + [pad8], axis=0).T.astype(BF16)

    sums[...] = jnp.zeros_like(sums)

    def lanes_of(chunk):
        return pl.ds(pl.multiple_of(chunk * W, W), W)

    def first_forward(chunk, _):
        here = lanes_of(chunk)
        d = geo[4:5, here]
        inverse_d = geo[5:6, here]
        x = d / cutoff
        x2 = x * x
        x3 = x2 * x
        x5 = x2 * x3
        x6 = x3 * x3
        envelope = 1.0 - 28.0 * x6 + 48.0 * x6 * x - 21.0 * x6 * x2
        slope = (-168.0 * x5 + 336.0 * x6 - 168.0 * x6 * x) / cutoff
        sine, cosine = sine_cosine(orders * x)
        even = scale * inverse_d * envelope
        values = sine * even
        slopes = cosine * (orders * (math.pi / cutoff)) * even + sine * (
            scale * inverse_d * (slope - envelope * inverse_d)
        )
        h, m, l = split3(jnp.concatenate([values, slopes], axis=1))
        start = jnp.concatenate([h, m, l, h, m, h], axis=0).astype(BF16)
        basis[chunk] = start
        pre = mm(one_in_s, start[:, 0:W])
        for layer, after in enumerate((one_mid0, one_mid1, one_out_s)):
            gate = logistic(pre)
            active = pre * gate
            slopes1[chunk, layer * RH : (layer + 1) * RH] = gate + active * (1.0 - gate)
            pre = mm(after, stack_right(active))
        radial1[...] = pre
        kind8 = jnp.concatenate(
            [(kinds == element[pl.ds(chunk * CH + j, 1), :]).astype(F32) for j in range(CH)], axis=1
        )
        picked_x = mm(lifted_s, jnp.concatenate([kind8, kind8, kind8, jnp.zeros_like(kind8)], axis=0).astype(BF16))
        total = [jnp.zeros((C, A), F32) for _ in range(4)]
        for j in range(CH):
            cut = slice(j * A, (j + 1) * A)
            at = pl.ds(pl.multiple_of(chunk * W + j * A, A), A)
            wx = picked_x[:, cut] * geo[3:4, at]
            total[0] += radial1[0:C, cut] * wx
            q1 = radial1[C : 2 * C, cut] * wx
            for a in range(3):
                total[a + 1] += geo[a : a + 1, at] * q1
            kept1[chunk, 0:C, cut] = q1
            kept1[chunk, C : 2 * C, cut] = wx
        for a in range(4):
            sums[a] += total[a]
        return 0

    def first_slopes(chunk, _):
        pre = mm(one_in_s, basis[chunk, :, W : 2 * W])
        for layer, after in enumerate((one_mid0, one_mid1, one_out_s)):
            pre = mm(after, stack_right(slopes1[chunk, layer * RH : (layer + 1) * RH] * pre))
        wx = kept1[chunk, C : 2 * C]
        kept1[chunk, C : 2 * C] = pre[0:C] * wx
        kept1[chunk, 2 * C : 3 * C] = pre[C : 2 * C] * wx
        return 0

    lax.fori_loop(0, NCH, first_forward, 0, unroll=True)

    s0 = mm(
        jnp.concatenate(list(split3(embedding[...])) + [pad8], axis=0).T.astype(BF16),
        jnp.concatenate([own_kind, own_kind, own_kind, pad8], axis=0).astype(BF16),
    )
    a0 = sums[0]
    a1 = [sums[1], sums[2], sums[3]]
    square = a1[0] * a1[0] + a1[1] * a1[1] + a1[2] * a1[2]
    s1 = s0 + mix(node_one[1], a0) + mix(node_one[2], a0 * a0) + mix(node_one[3], square)
    turned = mix(node_one[4], jnp.concatenate(a1, axis=1))
    gate1 = mix(node_one[5], a0)
    v1 = jnp.concatenate([turned[:, a * A : (a + 1) * A] + gate1 * a1[a] for a in range(3)], axis=1)
    lifted_x = mix(node_two[0], s1)
    lifted_y = mix(node_two[1], v1)
    own_table = jnp.concatenate([lifted_x] + [lifted_y[:, a * A : (a + 1) * A] for a in range(3)], axis=0)
    own_high, own_low = split2(own_table)
    send_a[...] = mm_nt(sent_rows, own_high) + mm_nt(sent_rows, own_low)
    table[:, 0:A] = own_high
    table[:, A : 2 * A] = own_low

    pl.semaphore_wait(barrier, 4 + many1 - 1 + many2 - 1)
    copies_a = exchange(0, lambda q: send_a.at[rows(q)], lambda q: recv_a.at[rows(q)])

    two_in_s = stack_basis(two_in[...])
    two_mid0, two_mid1 = stack_left(two_mid[0]), stack_left(two_mid[1])
    two_out_s = stack_out(two_out[...])

    def second_radial(chunk, _):
        row_of = lax.broadcasted_iota(jnp.int32, (EXT, A), 0)
        for j in range(CH):
            picked = neighbours[pl.ds(chunk * CH + j, 1), :]
            hot[chunk, :, j * A : (j + 1) * A] = (row_of == picked).astype(F32).astype(BF16)
        radial2[chunk] = radial_net(basis[chunk], two_in_s, two_mid0, two_mid1, two_out_s)
        own_hot = hot[chunk, 0:A, :]
        pairs[chunk] = mm(table[...], jnp.concatenate([own_hot, own_hot], axis=0))
        return 0

    lax.fori_loop(0, NCH, second_radial, 0, unroll=True)
    lax.fori_loop(0, NCH, first_slopes, 0, unroll=True)

    for copy in copies_a:
        copy.wait_recv()
    ghost_high, ghost_low = split2(recv_a[...].T)
    gather_parts[:, 0 : 4 * GH] = ghost_high
    gather_parts[:, 4 * GH : 8 * GH] = ghost_low

    sums2 = parts
    sums2[...] = jnp.zeros_like(sums2)

    def second_forward(chunk, _):
        far_hot = hot[chunk, A:EXT, :]
        pairs[chunk] += mm(gather_parts[...], jnp.concatenate([far_hot, far_hot], axis=0))
        total = [jnp.zeros((C, A), F32) for _ in range(4)]
        for j in range(CH):
            cut = slice(j * A, (j + 1) * A)
            at = pl.ds(chunk * W + j * A, A)
            w = geo[3:4, at]
            u = [geo[a : a + 1, at] for a in range(3)]
            wx = pairs[chunk, 0:C, cut] * w
            wy = [pairs[chunk, (a + 1) * C : (a + 2) * C, cut] * w for a in range(3)]
            along = wy[0] * u[0] + wy[1] * u[1] + wy[2] * u[2]
            total[0] += radial2[chunk, 0:C, cut] * wx + radial2[chunk, 3 * C : 4 * C, cut] * along
            r1x = radial2[chunk, C : 2 * C, cut] * wx
            r2 = radial2[chunk, 2 * C : 3 * C, cut]
            for a in range(3):
                total[a + 1] += r1x * u[a] + r2 * wy[a]
        for a in range(4):
            sums2[a] += total[a]
        return 0

    def all_second_forward(_, carry):
        for chunk in range(NCH):
            second_forward(chunk, 0)
        return carry

    lax.fori_loop(0, 1 + slab // slabs, all_second_forward, 0)

    b0 = sums2[0]
    b1 = [sums2[1], sums2[2], sums2[3]]
    square2 = b1[0] * b1[0] + b1[1] * b1[1] + b1[2] * b1[2]
    s2 = s1 + mix(node_two[2], b0) + mix(node_two[3], b0 * b0) + mix(node_two[4], square2)
    inner = jnp.concatenate([readout_hidden[...], jnp.zeros((C - 16, C), F32)], axis=0)
    pre = mix(inner, s2)
    gate2 = logistic(pre)
    hidden = pre * gate2
    shift = jnp.zeros((1, A), F32)
    mass = jnp.zeros((1, A), F32)
    for s in range(8):
        shift = jnp.where(species[...] == s, energy_shift[s], shift)
        mass = jnp.where(species[...] == s, masses[s], mass)
    packed_out[0:1, :] = (
        shift + jnp.sum(linear * s1, axis=0, keepdims=True) + jnp.sum(outer * hidden, axis=0, keepdims=True)
    )
    back_pre = outer * (gate2 + hidden * (1.0 - gate2))
    back_s2 = mix(inner.T, back_pre)
    back_b0 = mix(node_two[2].T, back_s2) + 2.0 * b0 * mix(node_two[3].T, back_s2)
    back_square2 = 2.0 * mix(node_two[4].T, back_s2)
    sums2[0] = back_b0
    for a in range(3):
        sums2[a + 1] = b1[a] * back_square2


    def second_back(side, chunk):
        for j in range(CH):
            cut = slice(j * A, (j + 1) * A)
            far = slice(W + j * A, W + (j + 1) * A)
            at = pl.ds(chunk * W + j * A, A)
            w = geo[3:4, at]
            wu = [w * geo[a : a + 1, at] for a in range(3)]
            r3 = radial2[chunk, 3 * C : 4 * C, cut]
            r2 = radial2[chunk, 2 * C : 3 * C, cut]

            def vector_part(a):
                return r3 * (sums2[0] * wu[a]) + r2 * (sums2[a + 1] * w)

            if side == 0:
                dot_u = sums2[1] * wu[0] + sums2[2] * wu[1] + sums2[3] * wu[2]
                back = [
                    radial2[chunk, 0:C, cut] * (sums2[0] * w) + radial2[chunk, C : 2 * C, cut] * dot_u,
                    vector_part(0),
                ]
            else:
                back = [vector_part(1), vector_part(2)]
            for a in range(2):
                h, l = split2(back[a])
                kept = slice(a * C, (a + 1) * C)
                packed[side, chunk, kept, cut] = h
                packed[side, chunk, kept, far] = l
        return mm_nt(hot[chunk], packed[side, chunk, :, 0:W]) + mm_nt(hot[chunk], packed[side, chunk, :, W : 2 * W])

    copies_b = []
    for side in range(2):
        half = pl.ds(side * 2 * C, 2 * C)
        gathered = second_back(side, 0)
        for chunk in range(1, NCH):
            gathered += second_back(side, chunk)
        scat[:, half] = gathered
        copies_b += exchange(
            1 + side, lambda q: scat.at[pl.ds(A + q * GH, GH), half], lambda q: recv_b.at[rows(q), half]
        )

    def second_edges(chunk, _):
        for j in range(CH):
            cut = slice(j * A, (j + 1) * A)
            far = slice(W + j * A, W + (j + 1) * A)
            at = pl.ds(pl.multiple_of(chunk * W + j * A, A), A)
            w = geo[3:4, at]
            u = [geo[a : a + 1, at] for a in range(3)]
            k0 = sums2[0]
            k1 = [sums2[a + 1] for a in range(3)]
            x = pairs[chunk, 0:C, cut]
            y = [pairs[chunk, (a + 1) * C : (a + 2) * C, cut] for a in range(3)]
            dot_u = k1[0] * u[0] + k1[1] * u[1] + k1[2] * u[2]
            along = y[0] * u[0] + y[1] * u[1] + y[2] * u[2]
            cross = y[0] * k1[0] + y[1] * k1[1] + y[2] * k1[2]
            stretch = (
                (radial2[chunk, 0:C, far] * k0 + radial2[chunk, C : 2 * C, far] * dot_u) * x
                + radial2[chunk, 3 * C : 4 * C, far] * along * k0
                + radial2[chunk, 2 * C : 3 * C, far] * cross
            )
            gflat[3:4, at] = w * jnp.sum(stretch, axis=0, keepdims=True)
            r3k0 = radial2[chunk, 3 * C : 4 * C, cut] * k0
            r1x = radial2[chunk, C : 2 * C, cut] * x
            for a in range(3):
                gflat[a : a + 1, at] = w * jnp.sum(r3k0 * y[a] + r1x * k1[a], axis=0, keepdims=True)
        return 0

    lax.fori_loop(0, NCH, second_edges, 0)

    for copy in copies_b:
        copy.wait_recv()
    back_high, back_low = split2(recv_b[...])
    back_table = (scat[0:A] + mm(sent_columns, back_high) + mm(sent_columns, back_low)).T
    back_s1 = back_s2 + linear + mix(node_two[0].T, back_table[0:C])
    back_v1 = mix(
        node_two[1].T, jnp.concatenate([back_table[(a + 1) * C : (a + 2) * C] for a in range(3)], axis=1)
    )
    back_turned = mix(node_one[4].T, back_v1)
    back_square = 2.0 * mix(node_one[3].T, back_s1)
    cut_v = [back_v1[:, a * A : (a + 1) * A] for a in range(3)]
    back_gate = a1[0] * cut_v[0] + a1[1] * cut_v[1] + a1[2] * cut_v[2]
    sums[0] = (
        mix(node_one[1].T, back_s1) + 2.0 * a0 * mix(node_one[2].T, back_s1) + mix(node_one[5].T, back_gate)
    )
    for a in range(3):
        sums[a + 1] = back_turned[:, a * A : (a + 1) * A] + gate1 * cut_v[a] + a1[a] * back_square

    push[...] = jnp.zeros_like(push)

    def first_edges(chunk, _):
        pieces = []
        for j in range(CH):
            cut = slice(j * A, (j + 1) * A)
            at = pl.ds(pl.multiple_of(chunk * W + j * A, A), A)
            u = [geo[a : a + 1, at] for a in range(3)]
            inverse_d = geo[5:6, at]
            k1 = [sums[a + 1] for a in range(3)]
            q1 = kept1[chunk, 0:C, cut]
            dot_u = k1[0] * u[0] + k1[1] * u[1] + k1[2] * u[2]
            stretch = gflat[3:4, at] + jnp.sum(
                kept1[chunk, C : 2 * C, cut] * sums[0] + kept1[chunk, 2 * C : 3 * C, cut] * dot_u,
                axis=0,
                keepdims=True,
            )
            turn = [gflat[a : a + 1, at] + jnp.sum(q1 * k1[a], axis=0, keepdims=True) for a in range(3)]
            inward = turn[0] * u[0] + turn[1] * u[1] + turn[2] * u[2]
            radial_part = stretch - inward * inverse_d
            for a in range(3):
                gflat[a : a + 1, at] = radial_part * u[a] + turn[a] * inverse_d
            gflat[3:8, at] = jnp.zeros((5, A), F32)
        g = gflat[:, lanes_of(chunk)]
        g_high = g.astype(BF16).astype(F32)
        both = jnp.concatenate([g_high, g - g_high], axis=0).astype(BF16)
        push[...] += mm_nt(hot[chunk], both)
        return 0

    lax.fori_loop(0, NCH, first_edges, 0, unroll=True)
    pushed = push[...]
    pushed = pushed[:, 0:8] + pushed[:, 8:16]
    push[:, 0:8] = pushed
    copies_c = exchange(3, lambda q: push.at[pl.ds(A + q * GH, GH)], lambda q: recv_c.at[rows(q)])

    own = jnp.zeros((8, A), F32)
    virial = [[jnp.zeros((1, A), F32) for _ in range(3)] for _ in range(3)]
    for k in range(K):
        own += gflat[:, k * A : (k + 1) * A]
        for a in range(3):
            for b in range(3):
                virial[a][b] += edges[a, k : k + 1, :] * gflat[b : b + 1, k * A : (k + 1) * A]
    for copy in copies_c:
        copy.wait_recv()
    come_high, come_low = split2(recv_c[...])
    back_f = (push[0:A] + mm(sent_columns, come_high) + mm(sent_columns, come_low)).T
    forces = own[0:3] - back_f[0:3]
    packed_out[8:11, :] = forces
    new_velocities = velocities[...] + time_step * forces / mass
    packed_out[16:19, :] = new_velocities

    order = (1, 0, 3, 2)
    movers = jnp.full((1, A), -1, jnp.int32)
    for q in range(4):
        for j in range(4):
            movers = jnp.where(lane == 4 * q + j, migrants[order[q], j], movers)
    chosen = (lax.broadcasted_iota(jnp.int32, (A, A), 0) == movers).astype(F32).astype(BF16)
    state = jnp.concatenate([positions[...], new_velocities, jnp.zeros((2, A), F32)], axis=0)
    h, m, l = split3(state)
    sent_state = mm(jnp.concatenate([h, m, l, jnp.zeros_like(h)], axis=0).astype(BF16), chosen)
    send_d[...] = sent_state[0:8] + sent_state[8:16] + sent_state[16:24]
    copies_d = exchange(4, lambda q: send_d, lambda q: recv_d.at[q])

    mine = jnp.zeros((1, A), F32)
    for a in range(3):
        for b in range(3):
            term = new_velocities[a : a + 1] * mass * new_velocities[b : b + 1] - virial[a][b]
            mine = jnp.where(lane == 3 * a + b, jnp.sum(term, axis=1, keepdims=True), mine)

    def all_sum(number, value, part, stage, many, me, peer, ring):
        part[...] = value.reshape(1, 1, A)
        stage[pl.ds(me, 1)] = value.reshape(1, 1, A)

        for step in sorted(range(1, many), key=lambda step: -min(step % ring, ring - step % ring)):
            pltpu.make_async_remote_copy(
                src_ref=part,
                dst_ref=stage.at[pl.ds(me, 1)],
                send_sem=sum_send.at[number],
                recv_sem=sum_recv.at[number],
                device_id=peer(step),
                device_id_type=MESH,
            ).start()

        whole = stage.at[pl.ds(0, many - 1)]
        pltpu.make_async_copy(whole, whole, sum_recv.at[number]).wait()
        pltpu.make_async_copy(whole, whole, sum_send.at[number]).wait()
        return jnp.sum(stage[...], axis=0)

    near = all_sum(0, mine, part1, stage1, many1, mine1, first_peer, subs)
    stress_row = all_sum(1, near, part2, stage2, many2, high, second_peer, many2)

    def entry(ref, a, b):
        return jnp.full((1, A), ref[a, b], F32)

    def determinant(m):
        return (
            m[0][0] * (m[1][1] * m[2][2] - m[1][2] * m[2][1])
            - m[0][1] * (m[1][0] * m[2][2] - m[1][2] * m[2][0])
            + m[0][2] * (m[1][0] * m[2][1] - m[1][1] * m[2][0])
        )

    def inverse(m):
        det = determinant(m)
        cof = [
            [
                m[(r + 1) % 3][(c + 1) % 3] * m[(r + 2) % 3][(c + 2) % 3]
                - m[(r + 1) % 3][(c + 2) % 3] * m[(r + 2) % 3][(c + 1) % 3]
                for c in range(3)
            ]
            for r in range(3)
        ]
        return [[cof[c][r] / det for c in range(3)] for r in range(3)]

    box = [[entry(box_matrix, a, b) for b in range(3)] for a in range(3)]
    volume = determinant(box)
    inv = inverse(box)
    total_atoms = box_mass * (A * slabs * subs)
    pressed = []
    for a in range(3):
        line = []
        for b in range(3):
            value = jnp.broadcast_to(stress_row[:, 3 * a + b : 3 * a + b + 1], (1, A))
            line.append(value - outside_pressure * volume if a == b else value)
        pressed.append(line)
    box_speed = []
    for a in range(3):
        line = []
        for b in range(3):
            pushed_box = pressed[a][0] * inv[b][0] + pressed[a][1] * inv[b][1] + pressed[a][2] * inv[b][2]
            line.append(entry(box_velocity, a, b) + time_step * pushed_box / total_atoms)
        box_speed.append(line)
    new_box = [[box[a][b] + time_step * box_speed[a][b] for b in range(3)] for a in range(3)]
    new_inverse = inverse(new_box)
    for group_at, matrix in ((40, new_box), (48, box_speed)):
        for a in range(3):
            line = jnp.where(lane == 0, matrix[a][0], jnp.where(lane == 1, matrix[a][1], matrix[a][2]))
            packed_out[group_at + a : group_at + a + 1, :] = line

    def drift(moving):
        return [
            new_inverse[a][0] * moving[0:1] + new_inverse[a][1] * moving[1:2] + new_inverse[a][2] * moving[2:3]
            for a in range(3)
        ]

    moved = drift(new_velocities)
    for a in range(3):
        packed_out[24 + a : 25 + a, :] = positions[a : a + 1, :] + time_step * moved[a]
    for copy in copies_d:
        copy.wait_recv()
    come = jnp.where(
        lane < 4, recv_d[0], jnp.where(lane < 8, recv_d[1], jnp.where(lane < 12, recv_d[2], recv_d[3]))
    )
    moved = drift(come[3:6])
    for a in range(3):
        packed_out[32 + a : 33 + a, :] = come[a : a + 1] + time_step * moved[a]
    packed_out[35:38, :] = come[3:6]

    for copies in (copies_a, copies_b, copies_c, copies_d):
        for copy in copies:
            copy.wait_send()


def unpack(held, *outs):
    for i, out in enumerate(outs):
        out[...] = held[8 * i : 8 * i + out.shape[0], 0 : out.shape[1]]


def solution(mesh):
    slabs, subs = mesh.shape["slab"], mesh.shape["sub"]
    many1, many2 = LO * subs, slabs // LO
    vmem = pl.BlockSpec(memory_space=pltpu.VMEM)
    smem = pl.BlockSpec(memory_space=pltpu.SMEM)
    in_smem = {9, 11, 12, 24, 25}

    def body(*arrays):
        arrays = list(arrays)
        for position in (2, 3, 21, 23):
            arrays[position] = arrays[position].reshape(1, -1)
        for position in (13, 15, 17, 19):
            arrays[position] = arrays[position].T
        shapes = [(1, A), (3, A), (3, A), (3, A), (6, 16), (3, 3), (3, 3)]
        held = pl.pallas_call(
            functools.partial(kernel, slabs, subs),
            out_shape=jax.ShapeDtypeStruct((8 * len(shapes), A), F32),
            in_specs=[smem if i in in_smem else vmem for i in range(26)],
            out_specs=vmem,
            scratch_shapes=[
                pltpu.VMEM((8, 128), F32),
                pltpu.VMEM((8, E), F32),
                pltpu.VMEM((K, A), jnp.int32),
                pltpu.VMEM((NCH, 48, 2 * W), BF16),
                pltpu.VMEM((NCH, EXT, W), BF16),
                pltpu.VMEM((NCH, 3 * C, W), F32),
                pltpu.VMEM((NCH, 3 * RH, W), F32),
                pltpu.VMEM((2 * C, W), F32),
                pltpu.VMEM((NCH, 4 * C, 2 * W), F32),
                pltpu.VMEM((4, C, A), F32),
                pltpu.VMEM((NCH, 4 * C, W), F32),
                pltpu.VMEM((4 * C, 2 * A), BF16),
                pltpu.VMEM((4, C, A), F32),
                pltpu.VMEM((4 * C, 8 * GH), BF16),
                pltpu.VMEM((2, NCH, 2 * C, 2 * W), BF16),
                pltpu.VMEM((8, E), F32),
                pltpu.VMEM((4 * GH, 4 * C), F32),
                pltpu.VMEM((4 * GH, 4 * C), F32),
                pltpu.VMEM((EXT, 4 * C), F32),
                pltpu.VMEM((4 * GH, 4 * C), F32),
                pltpu.VMEM((EXT, 16), F32),
                pltpu.VMEM((4 * GH, 16), F32),
                pltpu.VMEM((8, A), F32),
                pltpu.VMEM((4, 8, A), F32),
                pltpu.VMEM((many1, 1, A), F32),
                pltpu.VMEM((many2, 1, A), F32),
                pltpu.VMEM((1, 1, A), F32),
                pltpu.VMEM((1, 1, A), F32),
                pltpu.SemaphoreType.DMA((5, 4)),
                pltpu.SemaphoreType.DMA((5, 4)),
                pltpu.SemaphoreType.DMA((2,)),
                pltpu.SemaphoreType.DMA((2,)),
            ],
            compiler_params=pltpu.CompilerParams(
                collective_id=0, has_side_effects=True, vmem_limit_bytes=56 * 1024 * 1024
            ),
            name="step",
        )(*arrays)
        outs = pl.pallas_call(
            unpack,
            out_shape=[jax.ShapeDtypeStruct(shape, F32) for shape in shapes],
            in_specs=[vmem],
            out_specs=[vmem] * 7,
            name="unpack",
        )(held)
        return (outs[0].reshape(A),) + tuple(outs[1:])

    tail = P(None, ("slab", "sub"))
    flat = P(("slab", "sub"))
    placed = (tail, tail, flat, flat, tail, tail, P(None, None, ("slab", "sub")), tail, tail, tail) + (P(),) * 16
    return jax.shard_map(
        body,
        mesh=mesh,
        in_specs=placed,
        out_specs=(flat, tail, tail, tail, tail, P(), P()),
        check_vma=False,
    )
```
